512 devices in a mesh: row: 16 (over y_hi, x, core), col: 32 (over y_lo, z).
Axes of the slice: x: 4, y: 4 (y_hi: 2, y_lo: 2; y = y_hi * 2 + y_lo), z: 16, core: 2. Of those that a mesh axis runs over, the one named last changes fastest.
Arguments:
- eri: bfloat16 [128, 40, 40, 4096], P('row', None, None, 'col'), may hold values from -6 to 6
- slot_tile: int32 [128], P('row'), may hold values from 0 to 225, as said below
- tile_mask: int32 [225], replicated, may hold values from 0 to 1, as said below
- coef_mu: bfloat16 [600, 8], replicated, may hold values from -0.25 to 0.25
- coef_lam: bfloat16 [1024, 8], P('col'), may hold values from -0.1875 to 0.1875
Outputs:
- half_mo: float32 [32, 4800], P('col', 'row')
The draws below stay inside these ranges and needn't reach their ends.
Inputs may be any that keep to these rules, and one draw needn't show every extreme that they name: `slot_tile`: each tile (a, b) with a <= b of the 15 x 15 grid, written a * 15 + b, stands in exactly one slot; every other slot holds 225. `tile_mask`: entries of tiles below the diagonal (a > b) are 0.
All inputs are finite; a program needn't handle non-finite values.
Results may differ from the reference program's by a relative error of at most 0.0003.
Values sent between devices are 32-bit elements; how exact they have to be, the bound alone decides.
A program may use at most 64 MiB of HBM per device.

```python
import jax
import jax.numpy as jnp
import numpy as np
from jax import lax

N = 600
OCC = 8
BT = 40
SW = 4
NB = 15
SLOTS = 128
LAM = 1024


def draw_slot_tile(key, part):
    key = jax.random.fold_in(key, 11)
    every_id = np.arange(NB * NB)
    upper_ids = every_id[every_id // NB <= every_id % NB]
    filler = np.full(SLOTS - upper_ids.size, NB * NB)
    listed = jnp.asarray(np.concatenate([upper_ids, filler]).astype(np.int32))
    order = jax.random.permutation(key, SLOTS)
    return jnp.zeros((SLOTS,), jnp.int32).at[order].set(listed)


def draw_tile_mask(key, part):
    key = jax.random.fold_in(key, 12)
    every_id = jnp.arange(NB * NB, dtype=jnp.int32)
    upper = every_id // NB <= every_id % NB
    chosen = jax.random.randint(key, (NB * NB,), 0, 4) > 0
    return jnp.where(upper & chosen, 1, 0).astype(jnp.int32)


def levels(rng, dims, shards, least, high):
    loudness = 1.0
    for axis_at, shards_of in shards:
        steps = jax.random.uniform(jax.random.fold_in(jax.random.fold_in(rng, 6), axis_at), (shards_of,), jnp.float32, least / len(shards), high / len(shards))
        loudness = loudness * jnp.repeat(jnp.exp(steps), dims[axis_at] // shards_of).reshape((-1,) + (1,) * (len(dims) - 1 - axis_at))
    return loudness


def noise(stream_key, shape, spread, most, cuts=(), kind=jnp.bfloat16):
    entries = jax.random.normal(stream_key, shape, jnp.float32) * spread
    if len(cuts) > 0:
        entries = levels(stream_key, shape, cuts, -0.22, 0.18) * entries
    return jnp.clip(entries, min=-most, max=most).astype(kind)


def setup_inputs(seed: int = 0) -> dict:
    splits = jax.random.split(jax.random.key(seed), 6)
    eri = noise(splits[0], (SLOTS, BT, BT, LAM * SW), 1.0, 6.0, ((0, 16), (3, 32)))
    slot_tile = draw_slot_tile(jax.random.fold_in(splits[5], 71), 0)
    tile_mask = draw_tile_mask(jax.random.fold_in(splits[5], 71), 0)
    coef_mu = noise(splits[3], (N, OCC), N ** -0.5, 0.25)
    coef_lam = noise(splits[4], (LAM, OCC), LAM ** -0.5, 0.1875, ((0, 32),))
    return dict(eri=eri, slot_tile=slot_tile, tile_mask=tile_mask, coef_mu=coef_mu, coef_lam=coef_lam)


def reference(eri, slot_tile, tile_mask, coef_mu, coef_lam):
    blocks = coef_mu.astype(jnp.float32).reshape(NB, BT, OCC)
    empty = jnp.zeros((OCC, N, LAM * SW), jnp.float32)

    def add_slot(half_sums, inputs):
        tile_data, tile_id = inputs
        mu_block = tile_id // NB
        nu_block = tile_id % NB
        keep_tile = (tile_id < NB * NB) & (tile_mask[jnp.minimum(tile_id, NB * NB - 1)] > 0)
        weight = keep_tile.astype(jnp.float32)
        mirror = weight * (mu_block < nu_block).astype(jnp.float32)
        mu_safe = jnp.minimum(mu_block, NB - 1).astype(jnp.int32)
        nu_safe = nu_block.astype(jnp.int32)
        coef_first = lax.dynamic_index_in_dim(blocks, mu_safe, 0, keepdims=False)
        coef_second = lax.dynamic_index_in_dim(blocks, nu_safe, 0, keepdims=False)
        tile_float = tile_data.astype(jnp.float32)
        direct = jnp.einsum("pi,pqx->iqx", coef_first, tile_float) * weight
        mirrored = jnp.einsum("qi,pqx->ipx", coef_second, tile_float) * mirror
        nu_start = (nu_safe * BT).astype(jnp.int32)
        current = lax.dynamic_slice_in_dim(half_sums, nu_start, BT, 1)
        half_sums = lax.dynamic_update_slice_in_dim(half_sums, current + direct, nu_start, 1)
        mu_start = (mu_safe * BT).astype(jnp.int32)
        current = lax.dynamic_slice_in_dim(half_sums, mu_start, BT, 1)
        half_sums = lax.dynamic_update_slice_in_dim(half_sums, current + mirrored, mu_start, 1)
        return half_sums, None

    half_sums, unused = lax.scan(add_slot, empty, (eri, slot_tile))
    shaped = half_sums.reshape(OCC, N, LAM, SW)
    result = jnp.einsum("lj,inls->jsin", coef_lam.astype(jnp.float32), shaped, precision=lax.Precision.HIGHEST)
    return result.reshape(OCC * SW, OCC * N)
```

```python
import functools

import jax
import jax.numpy as jnp
from jax import lax
from jax.experimental import pallas as pl
from jax.experimental.pallas import tpu as pltpu
from jax.sharding import PartitionSpec as P

MESH = pl.DeviceIdType.MESH
SW = 4
F32 = jnp.float32
BF16 = jnp.bfloat16


def spread_coefficients(tile_ref, mask_ref, coef_ref, blocks, left, slots, edge, occ, nb):
    width = slots * edge
    for b in range(nb):
        blocks[b, :, :edge] = coef_ref[:, b * edge : (b + 1) * edge].astype(F32)
    lane = lax.broadcasted_iota(jnp.int32, (1, width), 1) // edge
    direct_parts, mirror_parts = [], []
    direct_target = jnp.full((1, width), -1, jnp.int32)
    mirror_target = jnp.full((1, width), -1, jnp.int32)
    for s in range(slots):
        tile = tile_ref[s]
        first, second = tile // nb, tile % nb
        valid = tile < nb * nb
        keep = jnp.where(valid & (mask_ref[jnp.minimum(tile, nb * nb - 1)] > 0), 1, 0)
        weight = keep.astype(F32)
        mirror = jnp.where(first < second, weight, 0.0)
        direct_parts.append(blocks[jnp.minimum(first, nb - 1)][:, :edge] * weight)
        mirror_parts.append(blocks[second][:, :edge] * mirror)
        direct_target = jnp.where(lane == s, second, direct_target)
        mirror_target = jnp.where(lane == s, first, mirror_target)
    gathered = jnp.concatenate(direct_parts + mirror_parts, axis=1)
    target = jnp.concatenate([direct_target, mirror_target], axis=1)
    row = lax.broadcasted_iota(jnp.int32, (8, 2 * width), 0)
    for half in range(2):
        for core in range(2):
            block = row + core * (8 - half)
            hit = target == block
            rows = []
            for i in range(occ):
                rows.append(jnp.where(hit, gathered[i : i + 1, :], 0.0).astype(BF16))
            left[half, pl.ds(core * 8 * occ, 8 * occ), :] = jnp.concatenate(rows, axis=0)


def kernel(
    eri_ref, tile_ref, mask_ref, coef_ref, lam_ref, out_ref,
    ebuf, eturn, blocks, left, acc, theirs, mine, got_core, send_plane, got_plane, send_z, got_z,
    load_sem, core_send, core_recv, plane_send, plane_recv, z_send, z_recv,
):
    slots, edge, unused, pairs = eri_ref.shape
    occ, basis = coef_ref.shape
    nb = basis // edge
    half_edge = edge // 2
    lams = lam_ref.shape[1]
    row, col = lax.axis_index("row"), lax.axis_index("col")
    core, orbital = row % 2, row // 2
    jhi, z = col // 16, col % 16
    place = orbital * 2 + jhi

    load = pltpu.make_async_copy(eri_ref, ebuf, load_sem)
    load.start()

    barrier = pltpu.get_barrier_semaphore()
    pl.semaphore_signal(barrier, inc=1, device_id=(orbital * 2 + 1 - core, col), device_id_type=MESH)

    def greet(d, unused):
        other = place ^ d
        pl.semaphore_signal(
            barrier, inc=1, device_id=((other // 2) * 2 + core, (other % 2) * 16 + z), device_id_type=MESH
        )
        pl.semaphore_signal(barrier, inc=1, device_id=(row, jhi * 16 + (z ^ d)), device_id_type=MESH)
        return unused

    lax.fori_loop(1, 16, greet, 0)

    spread_coefficients(tile_ref, mask_ref, coef_ref, blocks, left, slots, edge, occ, nb)

    rows_l = lax.broadcasted_iota(jnp.int32, (lams, pairs), 0)
    cols_l = lax.broadcasted_iota(jnp.int32, (lams, pairs), 1)
    widen = jnp.where(rows_l == cols_l // SW, 1.0, 0.0).astype(BF16)
    by_pair = jnp.dot(lam_ref[...], widen, preferred_element_type=F32)
    rows_j = lax.broadcasted_iota(jnp.int32, (occ * SW, occ), 0)
    cols_j = lax.broadcasted_iota(jnp.int32, (occ * SW, occ), 1)
    repeat = jnp.where(rows_j // SW == cols_j, 1.0, 0.0).astype(BF16)
    by_row = jnp.dot(repeat, by_pair.astype(BF16), preferred_element_type=F32)
    rows_s = lax.broadcasted_iota(jnp.int32, (occ * SW, pairs), 0)
    cols_s = lax.broadcasted_iota(jnp.int32, (occ * SW, pairs), 1)
    lam_mat = jnp.where(rows_s % SW == cols_s % SW, by_row, 0.0).astype(BF16)
    lam_twice = jnp.concatenate([lam_mat, lam_mat], axis=1)

    load.wait()
    for s in range(slots):
        eturn[:, s * edge : (s + 1) * edge, :] = jnp.swapaxes(ebuf[s], 0, 1)

    def transform(step, unused):
        for half in range(2):
            at = [step * 2, step * 2 + 1]
            right = jnp.concatenate(
                [
                    jnp.concatenate(
                        [eturn[half * half_edge + u], ebuf[:, half * half_edge + u].reshape(slots * edge, pairs)], axis=0
                    )
                    for u in at
                ],
                axis=1,
            )
            sums = jnp.dot(left[half], right, preferred_element_type=F32)
            for n, u in enumerate(at):
                for c in range(2):
                    start = (half ^ c) * half_edge + u
                    for i in range(occ):
                        g = c * occ + i
                        acc[g, pl.ds(start, 8, stride=edge), :] = sums[g * 8 : g * 8 + 8, n * pairs : (n + 1) * pairs]
        return unused

    lax.fori_loop(0, half_edge // 2, transform, 0)

    def contract(c, i):
        value = acc[c * occ + i]
        high = value.astype(BF16)
        low = (value - high.astype(F32)).astype(BF16)
        both = jnp.concatenate([high, low], axis=1)
        got = lax.dot_general(lam_twice, both, (((1,), (1,)), ((), ())), preferred_element_type=F32)
        return jnp.concatenate([got, jnp.zeros((occ * SW, 64), F32)], axis=1)

    pl.semaphore_wait(barrier, 31)
    core_copies = []
    for i in range(occ):
        got = contract(1 - core, i)
        theirs[2 * i] = got[:16]
        theirs[2 * i + 1] = got[16:]
        copy = pltpu.make_async_remote_copy(
            src_ref=theirs.at[pl.ds(2 * i, 2)],
            dst_ref=got_core.at[pl.ds(2 * i, 2)],
            send_sem=core_send.at[i],
            recv_sem=core_recv.at[i],
            device_id=(orbital * 2 + 1 - core, col),
            device_id_type=MESH,
        )
        copy.start()
        core_copies.append(copy)
    for i in range(occ):
        got = contract(core, i)
        mine[2 * i] = got[:16]
        mine[2 * i + 1] = got[16:]
    for copy in core_copies:
        copy.wait()

    plane_copies = []
    for d in range(1, 16):
        other = place ^ d
        send_plane[d] = mine[other] + got_core[other]
        copy = pltpu.make_async_remote_copy(
            src_ref=send_plane.at[d],
            dst_ref=got_plane.at[d],
            send_sem=plane_send.at[d],
            recv_sem=plane_recv.at[d],
            device_id=((other // 2) * 2 + core, (other % 2) * 16 + z),
            device_id_type=MESH,
        )
        copy.start()
        plane_copies.append(copy)
    total = mine[place] + got_core[place]
    for d in range(1, 16):
        plane_copies[d - 1].wait()
        total = total + got_plane[d]

    for k in range(3):
        send_z[:, k, :] = total[:, k * 128 : (k + 1) * 128]
    z_copies = []
    for d in range(1, 16):
        copy = pltpu.make_async_remote_copy(
            src_ref=send_z.at[z ^ d],
            dst_ref=got_z.at[d],
            send_sem=z_send.at[d],
            recv_sem=z_recv.at[d],
            device_id=(row, jhi * 16 + (z ^ d)),
            device_id_type=MESH,
        )
        copy.start()
        z_copies.append(copy)
    final = send_z[z]
    for d in range(1, 16):
        z_copies[d - 1].wait()
        final = final + got_z[d]
    out_ref[...] = final


def per_device(eri, slot_tile, tile_mask, coef_mu, coef_lam):
    slots, edge, unused, pairs = eri.shape
    basis, occ = coef_mu.shape
    nb = basis // edge
    smem = pl.BlockSpec(memory_space=pltpu.SMEM)
    vmem = pl.BlockSpec(memory_space=pltpu.VMEM)
    result = pl.pallas_call(
        kernel,
        out_shape=jax.ShapeDtypeStruct((3, 128), F32),
        in_specs=[pl.BlockSpec(memory_space=pl.ANY), smem, smem, vmem, vmem],
        out_specs=vmem,
        scratch_shapes=[
            pltpu.VMEM((slots, edge, edge, pairs), BF16),
            pltpu.VMEM((edge, slots * edge, pairs), BF16),
            pltpu.VMEM((nb, occ, 128), F32),
            pltpu.VMEM((2, 16 * occ, 2 * slots * edge), BF16),
            pltpu.VMEM((2 * occ, 8 * edge, pairs), F32),
            pltpu.VMEM((16, 16, 384), F32),
            pltpu.VMEM((16, 16, 384), F32),
            pltpu.VMEM((16, 16, 384), F32),
            pltpu.VMEM((16, 16, 384), F32),
            pltpu.VMEM((16, 16, 384), F32),
            pltpu.VMEM((16, 3, 128), F32),
            pltpu.VMEM((16, 3, 128), F32),
            pltpu.SemaphoreType.DMA,
            pltpu.SemaphoreType.DMA((occ,)),
            pltpu.SemaphoreType.DMA((occ,)),
            pltpu.SemaphoreType.DMA((16,)),
            pltpu.SemaphoreType.DMA((16,)),
            pltpu.SemaphoreType.DMA((16,)),
            pltpu.SemaphoreType.DMA((16,)),
        ],
        compiler_params=pltpu.CompilerParams(
            collective_id=0, has_side_effects=True, vmem_limit_bytes=56 * 2**20
        ),
    )(eri, slot_tile, tile_mask, coef_mu.T, coef_lam.T)
    return result.reshape(1, 384)[:, :300]


def solution(mesh):
    in_specs = (P("row", None, None, "col"), P("row"), P(), P(), P("col", None))
    out_specs = P("col", "row")
    return jax.shard_map(
        per_device, mesh=mesh, in_specs=in_specs, out_specs=out_specs, check_vma=False
    )
```

```python
import functools

import jax
import jax.numpy as jnp
from jax import lax
from jax.experimental import pallas as pl
from jax.experimental.pallas import tpu as pltpu
from jax.sharding import PartitionSpec as P

MESH = pl.DeviceIdType.MESH
SW = 4
PLANE_HOPS = (0, 1, 2, 1)
PLANE_ORDER = sorted(
    range(1, 16), key=lambda d: -(PLANE_HOPS[d // 8 * 2 + d % 2] + PLANE_HOPS[d // 2 % 4])
)
Z_ORDER = [8, 7, 9, 6, 10, 5, 11, 4, 12, 3, 13, 2, 14, 1, 15]
F32 = jnp.float32
BF16 = jnp.bfloat16


def spread_coefficients(tile_ref, mask_ref, coef_ref, blocks, left, slots, edge, occ, nb):
    width = slots * edge
    for b in range(nb):
        blocks[b, :, :edge] = coef_ref[:, b * edge : (b + 1) * edge].astype(F32)
    lane = lax.broadcasted_iota(jnp.int32, (1, width), 1) // edge
    direct_parts, mirror_parts = [], []
    direct_target = jnp.full((1, width), -1, jnp.int32)
    mirror_target = jnp.full((1, width), -1, jnp.int32)
    for s in range(slots):
        tile = tile_ref[s]
        first, second = tile // nb, tile % nb
        valid = tile < nb * nb
        keep = jnp.where(valid & (mask_ref[jnp.minimum(tile, nb * nb - 1)] > 0), 1, 0)
        weight = keep.astype(F32)
        mirror = jnp.where(first < second, weight, 0.0)
        direct_parts.append(blocks[jnp.minimum(first, nb - 1)][:, :edge] * weight)
        mirror_parts.append(blocks[second][:, :edge] * mirror)
        direct_target = jnp.where(lane == s, second, direct_target)
        mirror_target = jnp.where(lane == s, first, mirror_target)
    gathered = jnp.concatenate(direct_parts + mirror_parts, axis=1)
    target = jnp.concatenate([direct_target, mirror_target], axis=1)
    row = lax.broadcasted_iota(jnp.int32, (8, 2 * width), 0)
    for half in range(2):
        for core in range(2):
            block = row + core * (8 - half)
            hit = target == block
            rows = []
            for i in range(occ):
                rows.append(jnp.where(hit, gathered[i : i + 1, :], 0.0).astype(BF16))
            left[half, pl.ds(core * 8 * occ, 8 * occ), :] = jnp.concatenate(rows, axis=0)


def kernel(
    eri_hbm, tile_hbm, mask_hbm, coef_hbm, lam_hbm, out_ref,
    tile_ref, mask_ref, coef_ref, lam_ref, ebuf, eturn, blocks, left, acc, theirs, mine, got_core, send_plane, got_plane, send_z, got_z,
    load_sem, small_sem, core_send, core_recv, plane_send, plane_recv, z_send, z_recv,
):
    slots, edge, unused, pairs = ebuf.shape
    occ, basis = coef_ref.shape
    nb = basis // edge
    half_edge = edge // 2
    lams = lam_ref.shape[1]
    row, col = lax.axis_index("row"), lax.axis_index("col")
    core, orbital = row % 2, row // 2
    jhi, z = col // 16, col % 16
    place = orbital * 2 + jhi

    smalls = [
        pltpu.make_async_copy(a, b, small_sem.at[n])
        for n, (a, b) in enumerate(
            [(tile_hbm, tile_ref), (mask_hbm, mask_ref), (coef_hbm, coef_ref), (lam_hbm, lam_ref)]
        )
    ]
    for copy in smalls:
        copy.start()
    loads = [pltpu.make_async_copy(eri_hbm.at[s], ebuf.at[s], load_sem.at[s]) for s in range(slots)]
    for copy in loads:
        copy.start()

    barrier = pltpu.get_barrier_semaphore()
    pl.semaphore_signal(barrier, inc=1, device_id=(orbital * 2 + 1 - core, col), device_id_type=MESH)

    def greet(d, unused):
        other = place ^ d
        pl.semaphore_signal(
            barrier, inc=1, device_id=((other // 2) * 2 + core, (other % 2) * 16 + z), device_id_type=MESH
        )
        pl.semaphore_signal(barrier, inc=1, device_id=(row, jhi * 16 + (z ^ d)), device_id_type=MESH)
        return unused

    lax.fori_loop(1, 16, greet, 0)

    for copy in smalls:
        copy.wait()
    spread_coefficients(tile_ref, mask_ref, coef_ref, blocks, left, slots, edge, occ, nb)

    rows_l = lax.broadcasted_iota(jnp.int32, (lams, pairs), 0)
    cols_l = lax.broadcasted_iota(jnp.int32, (lams, pairs), 1)
    widen = jnp.where(rows_l == cols_l // SW, 1.0, 0.0).astype(BF16)
    by_pair = jnp.dot(lam_ref[...], widen, preferred_element_type=F32)
    rows_j = lax.broadcasted_iota(jnp.int32, (occ * SW, occ), 0)
    cols_j = lax.broadcasted_iota(jnp.int32, (occ * SW, occ), 1)
    repeat = jnp.where(rows_j // SW == cols_j, 1.0, 0.0).astype(BF16)
    by_row = jnp.dot(repeat, by_pair.astype(BF16), preferred_element_type=F32)
    rows_s = lax.broadcasted_iota(jnp.int32, (occ * SW, pairs), 0)
    cols_s = lax.broadcasted_iota(jnp.int32, (occ * SW, pairs), 1)
    lam_mat = jnp.where(rows_s % SW == cols_s % SW, by_row, 0.0).astype(BF16)
    lam_twice = jnp.concatenate([lam_mat, lam_mat], axis=1)

    for s in range(slots):
        loads[s].wait()
        eturn[:, s * edge : (s + 1) * edge, :] = jnp.swapaxes(ebuf[s], 0, 1)

    for step in range(half_edge // 2):
        for half in range(2):
            at = [step * 2, step * 2 + 1]
            right = jnp.concatenate(
                [
                    jnp.concatenate(
                        [eturn[half * half_edge + u], ebuf[:, half * half_edge + u].reshape(slots * edge, pairs)], axis=0
                    )
                    for u in at
                ],
                axis=1,
            )
            sums = jnp.dot(left[half], right, preferred_element_type=F32)
            for n, u in enumerate(at):
                for c in range(2):
                    start = (half ^ c) * half_edge + u
                    for i in range(occ):
                        g = c * occ + i
                        acc[g, pl.ds(start, 8, stride=edge), :] = sums[g * 8 : g * 8 + 8, n * pairs : (n + 1) * pairs]

    def contract(c, i):
        value = acc[c * occ + i]
        high = value.astype(BF16)
        low = (value - high.astype(F32)).astype(BF16)
        both = jnp.concatenate([high, low], axis=1)
        got = lax.dot_general(lam_twice, both, (((1,), (1,)), ((), ())), preferred_element_type=F32)
        return jnp.concatenate([got, jnp.zeros((occ * SW, 64), F32)], axis=1)

    pl.semaphore_wait(barrier, 31)
    core_copies = []
    for i in range(occ):
        got = contract(1 - core, i)
        theirs[2 * i] = got[:16]
        theirs[2 * i + 1] = got[16:]
        copy = pltpu.make_async_remote_copy(
            src_ref=theirs.at[pl.ds(2 * i, 2)],
            dst_ref=got_core.at[pl.ds(2 * i, 2)],
            send_sem=core_send.at[i],
            recv_sem=core_recv.at[i],
            device_id=(orbital * 2 + 1 - core, col),
            device_id_type=MESH,
        )
        copy.start()
        core_copies.append(copy)
    for i in range(occ):
        got = contract(core, i)
        mine[2 * i] = got[:16]
        mine[2 * i + 1] = got[16:]
    for copy in core_copies:
        copy.wait()

    plane_copies = []
    for d in PLANE_ORDER:
        other = place ^ d
        send_plane[d] = mine[other] + got_core[other]
        copy = pltpu.make_async_remote_copy(
            src_ref=send_plane.at[d],
            dst_ref=got_plane.at[d],
            send_sem=plane_send.at[d],
            recv_sem=plane_recv.at[d],
            device_id=((other // 2) * 2 + core, (other % 2) * 16 + z),
            device_id_type=MESH,
        )
        copy.start()
        plane_copies.append(copy)
    total = mine[place] + got_core[place]
    for copy, d in zip(plane_copies, PLANE_ORDER):
        copy.wait_recv()
        total = total + got_plane[d]

    for k in range(3):
        send_z[:, k, :] = total[:, k * 128 : (k + 1) * 128]
    z_copies = []
    for d in Z_ORDER:
        copy = pltpu.make_async_remote_copy(
            src_ref=send_z.at[(z + d) % 16],
            dst_ref=got_z.at[d],
            send_sem=z_send.at[d],
            recv_sem=z_recv.at[d],
            device_id=(row, jhi * 16 + (z + d) % 16),
            device_id_type=MESH,
        )
        copy.start()
        z_copies.append(copy)
    final = send_z[z]
    for copy, d in zip(z_copies, Z_ORDER):
        copy.wait_recv()
        final = final + got_z[d]
    for k in range(3):
        width = min(128, 300 - 128 * k)
        out_ref[:, k * 128 : k * 128 + width] = final[k : k + 1, :width]
    for copy in plane_copies + z_copies:
        copy.wait_send()


def per_device(eri, slot_tile, tile_mask, coef_mu, coef_lam):
    slots, edge, unused, pairs = eri.shape
    basis, occ = coef_mu.shape
    nb = basis // edge
    return pl.pallas_call(
        kernel,
        out_shape=pltpu.VMEM((1, 300), F32),
        in_specs=[pl.BlockSpec(memory_space=pltpu.HBM)] * 5,
        out_specs=pl.BlockSpec(memory_space=pltpu.VMEM),
        scratch_shapes=[
            pltpu.SMEM(slot_tile.shape, jnp.int32),
            pltpu.SMEM(tile_mask.shape, jnp.int32),
            pltpu.VMEM((occ, basis), BF16),
            pltpu.VMEM((occ, coef_lam.shape[0]), BF16),
            pltpu.VMEM((slots, edge, edge, pairs), BF16),
            pltpu.VMEM((edge, slots * edge, pairs), BF16),
            pltpu.VMEM((nb, occ, 128), F32),
            pltpu.VMEM((2, 16 * occ, 2 * slots * edge), BF16),
            pltpu.VMEM((2 * occ, 8 * edge, pairs), F32),
            pltpu.VMEM((16, 16, 384), F32),
            pltpu.VMEM((16, 16, 384), F32),
            pltpu.VMEM((16, 16, 384), F32),
            pltpu.VMEM((16, 16, 384), F32),
            pltpu.VMEM((16, 16, 384), F32),
            pltpu.VMEM((16, 3, 128), F32),
            pltpu.VMEM((16, 3, 128), F32),
            pltpu.SemaphoreType.DMA((slots,)),
            pltpu.SemaphoreType.DMA((4,)),
            pltpu.SemaphoreType.DMA((occ,)),
            pltpu.SemaphoreType.DMA((occ,)),
            pltpu.SemaphoreType.DMA((16,)),
            pltpu.SemaphoreType.DMA((16,)),
            pltpu.SemaphoreType.DMA((16,)),
            pltpu.SemaphoreType.DMA((16,)),
        ],
        compiler_params=pltpu.CompilerParams(
            collective_id=0, has_side_effects=True, vmem_limit_bytes=56 * 2**20
        ),
    )(eri, slot_tile, tile_mask, coef_mu.T, coef_lam.T)


def solution(mesh):
    in_specs = (P("row", None, None, "col"), P("row"), P(), P(), P("col", None))
    out_specs = P("col", "row")
    return jax.shard_map(
        per_device, mesh=mesh, in_specs=in_specs, out_specs=out_specs, check_vma=False
    )
```

```python
import functools

import jax
import jax.numpy as jnp
from jax import lax
from jax.experimental import pallas as pl
from jax.experimental.pallas import tpu as pltpu
from jax.sharding import PartitionSpec as P

MESH = pl.DeviceIdType.MESH
SW = 4
PLANE_HOPS = (0, 1, 2, 1)
PLANE_ORDER = sorted(
    range(1, 16), key=lambda d: -(PLANE_HOPS[d // 8 * 2 + d % 2] + PLANE_HOPS[d // 2 % 4])
)
Z_ORDER = [8, 7, 9, 6, 10, 5, 11, 4, 12, 3, 13, 2, 14, 1, 15]
F32 = jnp.float32
BF16 = jnp.bfloat16


def spread_coefficients(tile_ref, mask_ref, coef_ref, blocks, left, slots, edge, occ, nb):
    width = slots * edge
    for b in range(nb):
        blocks[b, :, :edge] = coef_ref[:, b * edge : (b + 1) * edge].astype(F32)
    lane = lax.broadcasted_iota(jnp.int32, (1, width), 1) // edge
    direct_parts, mirror_parts = [], []
    direct_target = jnp.full((1, width), -1, jnp.int32)
    mirror_target = jnp.full((1, width), -1, jnp.int32)
    for s in range(slots):
        tile = tile_ref[s]
        first, second = tile // nb, tile % nb
        valid = tile < nb * nb
        keep = jnp.where(valid & (mask_ref[jnp.minimum(tile, nb * nb - 1)] > 0), 1, 0)
        weight = keep.astype(F32)
        mirror = jnp.where(first < second, weight, 0.0)
        direct_parts.append(blocks[jnp.minimum(first, nb - 1)][:, :edge] * weight)
        mirror_parts.append(blocks[second][:, :edge] * mirror)
        direct_target = jnp.where(lane == s, second, direct_target)
        mirror_target = jnp.where(lane == s, first, mirror_target)
    gathered = jnp.concatenate(direct_parts + mirror_parts, axis=1)
    target = jnp.concatenate([direct_target, mirror_target], axis=1)
    row = lax.broadcasted_iota(jnp.int32, (8, 2 * width), 0)
    for half in range(2):
        for core in range(2):
            block = row + core * (8 - half)
            hit = target == block
            rows = []
            for i in range(occ):
                rows.append(jnp.where(hit, gathered[i : i + 1, :], 0.0).astype(BF16))
            left[half, pl.ds(core * 8 * occ, 8 * occ), :] = jnp.concatenate(rows, axis=0)


def second_factor(lam_ref, pairs, occ):
    lams = lam_ref.shape[1]
    rows_l = lax.broadcasted_iota(jnp.int32, (lams, pairs), 0)
    cols_l = lax.broadcasted_iota(jnp.int32, (lams, pairs), 1)
    widen = jnp.where(rows_l == cols_l // SW, 1.0, 0.0).astype(BF16)
    by_pair = jnp.dot(lam_ref[...], widen, preferred_element_type=F32)
    rows_j = lax.broadcasted_iota(jnp.int32, (occ * SW, occ), 0)
    cols_j = lax.broadcasted_iota(jnp.int32, (occ * SW, occ), 1)
    repeat = jnp.where(rows_j // SW == cols_j, 1.0, 0.0).astype(BF16)
    by_row = jnp.dot(repeat, by_pair.astype(BF16), preferred_element_type=F32)
    rows_s = lax.broadcasted_iota(jnp.int32, (occ * SW, pairs), 0)
    cols_s = lax.broadcasted_iota(jnp.int32, (occ * SW, pairs), 1)
    lam_mat = jnp.where(rows_s % SW == cols_s % SW, by_row, 0.0).astype(BF16)
    return jnp.concatenate([lam_mat, lam_mat], axis=1)


def output_order(order, z, edge):
    shape = order.shape
    k = lax.broadcasted_iota(jnp.int32, shape, 0)
    n = lax.broadcasted_iota(jnp.int32, shape, 1)
    tile, lane = k // 128, k % 128
    block = lane % 8
    wide = (lane // 64) * (edge // 2) + (lane // 8) % 8 + 8 * tile
    narrow = (lane // 32) % 2 * (edge // 2) + (lane // 8) % 4 + 16
    narrow = jnp.where(lane // 64 == z // 8, narrow, -1024)
    column = block * edge + jnp.where(tile < 2, wide, narrow)
    order[...] = jnp.where(column == n, 1.0, 0.0).astype(BF16)


def kernel(
    eri_hbm, tile_hbm, mask_hbm, coef_hbm, lam_hbm, out_ref,
    tile_ref, mask_ref, coef_ref, lam_ref, ebuf, eturn, blocks, left, order, acc_a, acc_b, acc_c,
    theirs_p, theirs_q, mine_p, mine_q, core_p, core_q, send_p, send_q, got_p, got_q, send_z, got_z,
    load_sem, small_sem, core_send, core_recv, p_send, p_recv, q_send, q_recv, z_send, z_recv,
):
    slots, edge, unused, pairs = ebuf.shape
    occ, basis = coef_ref.shape
    nb = basis // edge
    half_edge = edge // 2
    row, col = lax.axis_index("row"), lax.axis_index("col")
    core, orbital = row % 2, row // 2
    jhi, z = col // 16, col % 16
    place = orbital * 2 + jhi
    sibling = (orbital * 2 + 1 - core, col)

    smalls = [
        pltpu.make_async_copy(a, b, small_sem.at[n])
        for n, (a, b) in enumerate(
            [(tile_hbm, tile_ref), (mask_hbm, mask_ref), (coef_hbm, coef_ref), (lam_hbm, lam_ref)]
        )
    ]
    for copy in smalls:
        copy.start()
    loads = [pltpu.make_async_copy(eri_hbm.at[s], ebuf.at[s], load_sem.at[s]) for s in range(slots)]
    for copy in loads:
        copy.start()

    barrier = pltpu.get_barrier_semaphore()
    pl.semaphore_signal(barrier, inc=1, device_id=sibling, device_id_type=MESH)

    def greet(d, unused):
        other = place ^ d
        pl.semaphore_signal(
            barrier, inc=1, device_id=((other // 2) * 2 + core, (other % 2) * 16 + z), device_id_type=MESH
        )
        pl.semaphore_signal(barrier, inc=1, device_id=(row, jhi * 16 + (z ^ d)), device_id_type=MESH)
        return unused

    lax.fori_loop(1, 16, greet, 0)

    output_order(order, z, edge)
    for copy in smalls:
        copy.wait()
    spread_coefficients(tile_ref, mask_ref, coef_ref, blocks, left, slots, edge, occ, nb)
    lam_twice = second_factor(lam_ref, pairs, occ)

    for s in range(slots):
        loads[s].wait()
        eturn[:, s * edge : (s + 1) * edge, :] = jnp.swapaxes(ebuf[s], 0, 1)

    def transform(acc, first, count):
        for half in range(2):
            for step in range(0, count, 2):
                base = half * half_edge + first + step
                right = jnp.concatenate(
                    [
                        jnp.concatenate([eturn[u], ebuf[:, u].reshape(slots * edge, pairs)], axis=0)
                        for u in (base, base + 1)
                    ],
                    axis=1,
                )
                sums = jnp.dot(left[half], right, preferred_element_type=F32)
                for c in range(2):
                    start = ((half ^ c) * count + step) * 8
                    for i in range(occ):
                        g = (c * occ + i) * 8
                        both = jnp.concatenate([sums[g : g + 8, :pairs], sums[g : g + 8, pairs:]], axis=0)
                        high = both.astype(BF16)
                        low = (both - high.astype(F32)).astype(BF16)
                        at = i * 2 * count * 8 + start
                        acc[c, at : at + 16, :pairs] = high
                        acc[c, at : at + 16, pairs:] = low

    def contract(acc, c, n):
        right = acc[c, n * 256 : n * 256 + 256, :]
        return lax.dot_general(lam_twice, right, (((1,), (1,)), ((), ())), preferred_element_type=F32)

    def contract_wide(acc, c, dest):
        for n in range(occ // 2):
            got = contract(acc, c, n)
            for k in range(2):
                for h in range(2):
                    dest[4 * n + 2 * k + h, 0:16, :] = got[16 * h : 16 * h + 16, 128 * k : 128 * k + 128]

    def contract_narrow(acc, c, dest):
        low_lanes = lax.broadcasted_iota(jnp.int32, (8, 128), 1) < 64
        for n in range(occ // 4):
            got = contract(acc, c, n)
            for k in range(2):
                for h in range(2):
                    below = got[16 * h : 16 * h + 8, 128 * k : 128 * k + 128]
                    above = got[16 * h + 8 : 16 * h + 16, 128 * k : 128 * k + 128]
                    m = 8 * n + 4 * k + h
                    dest[m, 16:24, :] = jnp.where(low_lanes, below, pltpu.roll(above, 64, 1))
                    dest[m + 2, 16:24, :] = jnp.where(low_lanes, pltpu.roll(below, 64, 1), above)

    def swap_cores(source, dest, n):
        copy = pltpu.make_async_remote_copy(
            src_ref=source, dst_ref=dest, send_sem=core_send.at[n], recv_sem=core_recv.at[n],
            device_id=sibling, device_id_type=MESH,
        )
        copy.start()
        return copy

    def share(mine, theirs, send, got, send_sem, recv_sem):
        copies = []
        for d in PLANE_ORDER:
            other = place ^ d
            send[d] = mine[other] + theirs[other]
            copy = pltpu.make_async_remote_copy(
                src_ref=send.at[d],
                dst_ref=got.at[d],
                send_sem=send_sem.at[d],
                recv_sem=recv_sem.at[d],
                device_id=((other // 2) * 2 + core, (other % 2) * 16 + z),
                device_id_type=MESH,
            )
            copy.start()
            copies.append(copy)
        return copies

    def gather(mine, theirs, got, copies):
        total = mine[place] + theirs[place]
        for copy, d in zip(copies, PLANE_ORDER):
            copy.wait_recv()
            total = total + got[d]
        return total

    transform(acc_a, 0, 8)
    contract_wide(acc_a, 1 - core, theirs_p)
    pl.semaphore_wait(barrier, 31)
    first_swap = swap_cores(theirs_p, core_p, 0)
    contract_wide(acc_a, core, mine_p)
    transform(acc_b, 8, 8)
    transform(acc_c, 16, 4)
    contract_wide(acc_b, 1 - core, theirs_q)
    contract_narrow(acc_c, 1 - core, theirs_q)
    second_swap = swap_cores(theirs_q, core_q, 1)
    first_swap.wait_recv()
    p_copies = share(mine_p, core_p, send_p, got_p, p_send, p_recv)
    contract_wide(acc_b, core, mine_q)
    contract_narrow(acc_c, core, mine_q)
    second_swap.wait_recv()
    q_copies = share(mine_q, core_q, send_q, got_q, q_send, q_recv)

    total = gather(mine_p, core_p, got_p, p_copies)
    send_z[:, 0, :] = total
    total = gather(mine_q, core_q, got_q, q_copies)
    send_z[:, 1, :] = total[:16]
    send_z[0:8, 2, :] = total[16:]
    send_z[8:16, 2, :] = total[16:]
    z_copies = []
    for d in Z_ORDER:
        other = (z + d) % 16
        copy = pltpu.make_async_remote_copy(
            src_ref=send_z.at[other],
            dst_ref=got_z.at[d],
            send_sem=z_send.at[d],
            recv_sem=z_recv.at[d],
            device_id=(row, jhi * 16 + other),
            device_id_type=MESH,
        )
        copy.start()
        z_copies.append(copy)
    final = send_z[z]
    for copy, d in zip(z_copies, Z_ORDER):
        copy.wait_recv()
        final = final + got_z[d]
    flat = jnp.concatenate([final[k : k + 1, :] for k in range(3)], axis=1)
    high = flat.astype(BF16)
    rest = flat - high.astype(F32)
    middle = rest.astype(BF16)
    low = (rest - middle.astype(F32)).astype(BF16)
    terms = jnp.concatenate([high, middle, low], axis=0)
    picked = jnp.dot(terms, order[...], preferred_element_type=F32)
    out_ref[...] = (picked[0:1] + picked[1:2] + picked[2:3])[:, : out_ref.shape[1]]
    for copy in [first_swap, second_swap] + p_copies + q_copies + z_copies:
        copy.wait_send()


def per_device(eri, slot_tile, tile_mask, coef_mu, coef_lam):
    slots, edge, unused, pairs = eri.shape
    basis, occ = coef_mu.shape
    nb = basis // edge
    return pl.pallas_call(
        kernel,
        out_shape=pltpu.VMEM((1, 300), F32),
        in_specs=[pl.BlockSpec(memory_space=pltpu.HBM)] * 5,
        out_specs=pl.BlockSpec(memory_space=pltpu.VMEM),
        scratch_shapes=[
            pltpu.SMEM(slot_tile.shape, jnp.int32),
            pltpu.SMEM(tile_mask.shape, jnp.int32),
            pltpu.VMEM((occ, basis), BF16),
            pltpu.VMEM((occ, coef_lam.shape[0]), BF16),
            pltpu.VMEM((slots, edge, edge, pairs), BF16),
            pltpu.VMEM((edge, slots * edge, pairs), BF16),
            pltpu.VMEM((nb, occ, 128), F32),
            pltpu.VMEM((2, 16 * occ, 2 * slots * edge), BF16),
            pltpu.VMEM((384, 384), BF16),
            pltpu.VMEM((2, occ * 128, 2 * pairs), BF16),
            pltpu.VMEM((2, occ * 128, 2 * pairs), BF16),
            pltpu.VMEM((2, occ * 64, 2 * pairs), BF16),
        ]
        + [pltpu.VMEM((16, height, 128), F32) for unused in range(5) for height in (16, 24)]
        + [
            pltpu.VMEM((16, 3, 128), F32),
            pltpu.VMEM((16, 3, 128), F32),
            pltpu.SemaphoreType.DMA((slots,)),
            pltpu.SemaphoreType.DMA((4,)),
            pltpu.SemaphoreType.DMA((2,)),
            pltpu.SemaphoreType.DMA((2,)),
            pltpu.SemaphoreType.DMA((16,)),
            pltpu.SemaphoreType.DMA((16,)),
            pltpu.SemaphoreType.DMA((16,)),
            pltpu.SemaphoreType.DMA((16,)),
            pltpu.SemaphoreType.DMA((16,)),
            pltpu.SemaphoreType.DMA((16,)),
        ],
        compiler_params=pltpu.CompilerParams(
            collective_id=0, has_side_effects=True, vmem_limit_bytes=56 * 2**20
        ),
    )(eri, slot_tile, tile_mask, coef_mu.T, coef_lam.T)


def solution(mesh):
    in_specs = (P("row", None, None, "col"), P("row"), P(), P(), P("col", None))
    out_specs = P("col", "row")
    return jax.shard_map(
        per_device, mesh=mesh, in_specs=in_specs, out_specs=out_specs, check_vma=False
    )
```

```python
import functools

import jax
import jax.numpy as jnp
from jax import lax
from jax.experimental import pallas as pl
from jax.experimental.pallas import tpu as pltpu
from jax.sharding import PartitionSpec as P

MESH = pl.DeviceIdType.MESH
SW = 4
PLANE_HOPS = (0, 1, 2, 1)
PLANE_ORDER = sorted(
    range(1, 16), key=lambda d: -(PLANE_HOPS[d // 8 * 2 + d % 2] + PLANE_HOPS[d // 2 % 4])
)
Z_ORDER = [8, 7, 9, 6, 10, 5, 11, 4, 12, 3, 13, 2, 14, 1, 15]
F32 = jnp.float32
BF16 = jnp.bfloat16


def spread_coefficients(tile_ref, mask_ref, coef_ref, blocks, left, slots, edge, occ, nb):
    width = slots * edge
    for b in range(nb):
        blocks[b, :, :edge] = coef_ref[:, b * edge : (b + 1) * edge].astype(F32)
    lane = lax.broadcasted_iota(jnp.int32, (1, width), 1) // edge
    direct_parts, mirror_parts = [], []
    direct_target = jnp.full((1, width), -1, jnp.int32)
    mirror_target = jnp.full((1, width), -1, jnp.int32)
    for s in range(slots):
        tile = tile_ref[s]
        first, second = tile // nb, tile % nb
        valid = tile < nb * nb
        keep = jnp.where(valid & (mask_ref[jnp.minimum(tile, nb * nb - 1)] > 0), 1, 0)
        weight = keep.astype(F32)
        mirror = jnp.where(first < second, weight, 0.0)
        direct_parts.append(blocks[jnp.minimum(first, nb - 1)][:, :edge] * weight)
        mirror_parts.append(blocks[second][:, :edge] * mirror)
        direct_target = jnp.where(lane == s, second, direct_target)
        mirror_target = jnp.where(lane == s, first, mirror_target)
    gathered = jnp.concatenate(direct_parts + mirror_parts, axis=1)
    target = jnp.concatenate([direct_target, mirror_target], axis=1)
    row = lax.broadcasted_iota(jnp.int32, (8, 2 * width), 0)
    for half in range(2):
        for core in range(2):
            block = row + core * (8 - half)
            hit = target == block
            rows = []
            for i in range(occ):
                rows.append(jnp.where(hit, gathered[i : i + 1, :], 0.0).astype(BF16))
            left[half, pl.ds(core * 8 * occ, 8 * occ), :] = jnp.concatenate(rows, axis=0)


def second_factor(lam_ref, pairs, occ):
    lams = lam_ref.shape[1]
    rows_l = lax.broadcasted_iota(jnp.int32, (lams, pairs), 0)
    cols_l = lax.broadcasted_iota(jnp.int32, (lams, pairs), 1)
    widen = jnp.where(rows_l == cols_l // SW, 1.0, 0.0).astype(BF16)
    by_pair = jnp.dot(lam_ref[...], widen, preferred_element_type=F32)
    rows_j = lax.broadcasted_iota(jnp.int32, (occ * SW, occ), 0)
    cols_j = lax.broadcasted_iota(jnp.int32, (occ * SW, occ), 1)
    repeat = jnp.where(rows_j // SW == cols_j, 1.0, 0.0).astype(BF16)
    by_row = jnp.dot(repeat, by_pair.astype(BF16), preferred_element_type=F32)
    rows_s = lax.broadcasted_iota(jnp.int32, (occ * SW, pairs), 0)
    cols_s = lax.broadcasted_iota(jnp.int32, (occ * SW, pairs), 1)
    lam_mat = jnp.where(rows_s % SW == cols_s % SW, by_row, 0.0).astype(BF16)
    return jnp.concatenate([lam_mat, lam_mat], axis=1)


def output_order(order, z, edge):
    shape = order.shape
    k = lax.broadcasted_iota(jnp.int32, shape, 0)
    n = lax.broadcasted_iota(jnp.int32, shape, 1)
    tile, lane = k // 128, k % 128
    block = lane % 8
    wide = (lane // 64) * (edge // 2) + (lane // 8) % 8 + 8 * tile
    narrow = (lane // 32) % 2 * (edge // 2) + (lane // 8) % 4 + 16
    narrow = jnp.where(lane // 64 == z // 8, narrow, -1024)
    column = block * edge + jnp.where(tile < 2, wide, narrow)
    order[...] = jnp.where(column == n, 1.0, 0.0).astype(BF16)


def kernel(
    eri_hbm, tile_hbm, mask_hbm, coef_hbm, lam_hbm, out_ref,
    tile_ref, mask_ref, coef_ref, lam_ref, ebuf, eturn, blocks, left, order, acc_a, acc_b, acc_c,
    theirs_p, theirs_q, mine_p, mine_q, core_p, core_q, send_p, send_q, got_p, got_q, send_z, got_z,
    load_sem, small_sem, core_send, core_recv, plane_send, plane_recv, z_send, z_recv,
):
    slots, edge, unused, pairs = ebuf.shape
    occ, basis = coef_ref.shape
    nb = basis // edge
    half_edge = edge // 2
    row, col = lax.axis_index("row"), lax.axis_index("col")
    core, orbital = row % 2, row // 2
    jhi, z = col // 16, col % 16
    place = orbital * 2 + jhi
    sibling = (orbital * 2 + 1 - core, col)

    smalls = [
        pltpu.make_async_copy(a, b, small_sem.at[n])
        for n, (a, b) in enumerate(
            [(tile_hbm, tile_ref), (mask_hbm, mask_ref), (coef_hbm, coef_ref), (lam_hbm, lam_ref)]
        )
    ]
    for copy in smalls:
        copy.start()
    loads = [pltpu.make_async_copy(eri_hbm.at[s], ebuf.at[s], load_sem.at[s]) for s in range(slots)]
    for copy in loads:
        copy.start()

    barrier = pltpu.get_barrier_semaphore()
    pl.semaphore_signal(barrier, inc=1, device_id=sibling, device_id_type=MESH)

    def greet(d, unused):
        other = place ^ d
        pl.semaphore_signal(
            barrier, inc=1, device_id=((other // 2) * 2 + core, (other % 2) * 16 + z), device_id_type=MESH
        )
        pl.semaphore_signal(barrier, inc=1, device_id=(row, jhi * 16 + (z ^ d)), device_id_type=MESH)
        return unused

    lax.fori_loop(1, 16, greet, 0)

    output_order(order, z, edge)
    for copy in smalls:
        copy.wait()
    spread_coefficients(tile_ref, mask_ref, coef_ref, blocks, left, slots, edge, occ, nb)
    lam_twice = second_factor(lam_ref, pairs, occ)

    for s in range(slots):
        loads[s].wait()
        eturn[:, s * edge : (s + 1) * edge, :] = jnp.swapaxes(ebuf[s], 0, 1)

    def transform(acc, first, count):
        for half in range(2):
            for step in range(0, count, 2):
                base = half * half_edge + first + step
                right = jnp.concatenate(
                    [
                        jnp.concatenate([eturn[u], ebuf[:, u].reshape(slots * edge, pairs)], axis=0)
                        for u in (base, base + 1)
                    ],
                    axis=1,
                )
                sums = jnp.dot(left[half], right, preferred_element_type=F32)
                for c in range(2):
                    start = ((half ^ c) * count + step) * 8
                    for i in range(occ):
                        g = (c * occ + i) * 8
                        at = i * 2 * count * 8 + start
                        acc[c, at : at + 8, :] = sums[g : g + 8, :pairs]
                        acc[c, at + 8 : at + 16, :] = sums[g : g + 8, pairs:]

    def contract(acc, c, n):
        value = acc[c, n * 256 : n * 256 + 256, :]
        high = value.astype(BF16)
        low = (value - high.astype(F32)).astype(BF16)
        right = jnp.concatenate([high, low], axis=1)
        return lax.dot_general(lam_twice, right, (((1,), (1,)), ((), ())), preferred_element_type=F32)

    def contract_wide(acc, c, dest):
        for n in range(occ // 2):
            got = contract(acc, c, n)
            for k in range(2):
                for h in range(2):
                    dest[4 * n + 2 * k + h, 0:16, :] = got[16 * h : 16 * h + 16, 128 * k : 128 * k + 128]

    def contract_narrow(acc, c, dest):
        low_lanes = lax.broadcasted_iota(jnp.int32, (8, 128), 1) < 64
        for n in range(occ // 4):
            got = contract(acc, c, n)
            for k in range(2):
                for h in range(2):
                    below = got[16 * h : 16 * h + 8, 128 * k : 128 * k + 128]
                    above = got[16 * h + 8 : 16 * h + 16, 128 * k : 128 * k + 128]
                    m = 8 * n + 4 * k + h
                    dest[m, 16:24, :] = jnp.where(low_lanes, below, pltpu.roll(above, 64, 1))
                    dest[m + 2, 16:24, :] = jnp.where(low_lanes, pltpu.roll(below, 64, 1), above)

    def swap_cores(source, dest, n):
        copy = pltpu.make_async_remote_copy(
            src_ref=source, dst_ref=dest, send_sem=core_send.at[n], recv_sem=core_recv.at[n],
            device_id=sibling, device_id_type=MESH,
        )
        copy.start()
        return copy

    def to_plane(send, got, n, slot, other):
        return pltpu.make_async_remote_copy(
            src_ref=send.at[slot],
            dst_ref=got.at[slot],
            send_sem=plane_send.at[n],
            recv_sem=plane_recv.at[n],
            device_id=((other // 2) * 2 + core, (other % 2) * 16 + z),
            device_id_type=MESH,
        )

    def share(mine, theirs, send, got, n):
        for d in PLANE_ORDER:
            other = place ^ d
            send[d] = mine[other] + theirs[other]
            to_plane(send, got, n, d, other).start()
        return to_plane(send, got, n, pl.ds(1, 15), place ^ 1)

    def gather(mine, theirs, got, copies):
        total = mine[place] + theirs[place]
        copies.wait_recv()
        for d in range(1, 16):
            total = total + got[d]
        return total

    transform(acc_a, 0, 8)
    contract_wide(acc_a, 1 - core, theirs_p)
    pl.semaphore_wait(barrier, 31)
    first_swap = swap_cores(theirs_p, core_p, 0)
    contract_wide(acc_a, core, mine_p)
    transform(acc_b, 8, 8)
    transform(acc_c, 16, 4)
    contract_wide(acc_b, 1 - core, theirs_q)
    contract_narrow(acc_c, 1 - core, theirs_q)
    second_swap = swap_cores(theirs_q, core_q, 1)
    first_swap.wait_recv()
    p_copies = share(mine_p, core_p, send_p, got_p, 0)
    contract_wide(acc_b, core, mine_q)
    contract_narrow(acc_c, core, mine_q)
    second_swap.wait_recv()
    q_copies = share(mine_q, core_q, send_q, got_q, 1)

    total = gather(mine_p, core_p, got_p, p_copies)
    send_z[:, 0, :] = total
    total = gather(mine_q, core_q, got_q, q_copies)
    send_z[:, 1, :] = total[:16]
    send_z[0:8, 2, :] = total[16:]
    send_z[8:16, 2, :] = total[16:]

    def along_z(source, slot, other):
        return pltpu.make_async_remote_copy(
            src_ref=send_z.at[source],
            dst_ref=got_z.at[slot],
            send_sem=z_send,
            recv_sem=z_recv,
            device_id=(row, jhi * 16 + other),
            device_id_type=MESH,
        )

    for d in Z_ORDER:
        other = (z + d) % 16
        along_z(other, d, other).start()
    z_copies = along_z(pl.ds(1, 15), pl.ds(1, 15), (z + 1) % 16)
    final = send_z[z]
    z_copies.wait_recv()
    for d in range(1, 16):
        final = final + got_z[d]
    flat = jnp.concatenate([final[k : k + 1, :] for k in range(3)], axis=1)
    high = flat.astype(BF16)
    rest = flat - high.astype(F32)
    middle = rest.astype(BF16)
    low = (rest - middle.astype(F32)).astype(BF16)
    terms = jnp.concatenate([high, middle, low], axis=0)
    picked = jnp.dot(terms, order[...], preferred_element_type=F32)
    out_ref[...] = (picked[0:1] + picked[1:2] + picked[2:3])[:, : out_ref.shape[1]]
    for copy in (first_swap, second_swap, p_copies, q_copies, z_copies):
        copy.wait_send()


def per_device(eri, slot_tile, tile_mask, coef_mu, coef_lam):
    slots, edge, unused, pairs = eri.shape
    basis, occ = coef_mu.shape
    nb = basis // edge
    return pl.pallas_call(
        kernel,
        out_shape=pltpu.VMEM((1, 300), F32),
        in_specs=[pl.BlockSpec(memory_space=pltpu.HBM)] * 5,
        out_specs=pl.BlockSpec(memory_space=pltpu.VMEM),
        scratch_shapes=[
            pltpu.SMEM(slot_tile.shape, jnp.int32),
            pltpu.SMEM(tile_mask.shape, jnp.int32),
            pltpu.VMEM((occ, basis), BF16),
            pltpu.VMEM((occ, coef_lam.shape[0]), BF16),
            pltpu.VMEM((slots, edge, edge, pairs), BF16),
            pltpu.VMEM((edge, slots * edge, pairs), BF16),
            pltpu.VMEM((nb, occ, 128), F32),
            pltpu.VMEM((2, 16 * occ, 2 * slots * edge), BF16),
            pltpu.VMEM((384, 384), BF16),
            pltpu.VMEM((2, occ * 128, pairs), F32),
            pltpu.VMEM((2, occ * 128, pairs), F32),
            pltpu.VMEM((2, occ * 64, pairs), F32),
        ]
        + [pltpu.VMEM((16, height, 128), F32) for unused in range(5) for height in (16, 24)]
        + [
            pltpu.VMEM((16, 3, 128), F32),
            pltpu.VMEM((16, 3, 128), F32),
            pltpu.SemaphoreType.DMA((slots,)),
            pltpu.SemaphoreType.DMA((4,)),
            pltpu.SemaphoreType.DMA((2,)),
            pltpu.SemaphoreType.DMA((2,)),
            pltpu.SemaphoreType.DMA((2,)),
            pltpu.SemaphoreType.DMA((2,)),
            pltpu.SemaphoreType.DMA,
            pltpu.SemaphoreType.DMA,
        ],
        compiler_params=pltpu.CompilerParams(
            collective_id=0, has_side_effects=True, vmem_limit_bytes=56 * 2**20
        ),
    )(eri, slot_tile, tile_mask, coef_mu.T, coef_lam.T)


def solution(mesh):
    in_specs = (P("row", None, None, "col"), P("row"), P(), P(), P("col", None))
    out_specs = P("col", "row")
    return jax.shard_map(
        per_device, mesh=mesh, in_specs=in_specs, out_specs=out_specs, check_vma=False
    )
```

```python
import functools

import jax
import jax.numpy as jnp
from jax import lax
from jax.experimental import pallas as pl
from jax.experimental.pallas import tpu as pltpu
from jax.sharding import PartitionSpec as P

MESH = pl.DeviceIdType.MESH
SW = 4
PLANE_HOPS = (0, 1, 2, 1)
PLANE_ORDER = sorted(
    range(1, 16), key=lambda d: -(PLANE_HOPS[d // 8 * 2 + d % 2] + PLANE_HOPS[d // 2 % 4])
)
Z_ORDER = [8, 7, 9, 6, 10, 5, 11, 4, 12, 3, 13, 2, 14, 1, 15]
F32 = jnp.float32
BF16 = jnp.bfloat16


def spread_coefficients(tile_ref, mask_ref, coef_ref, blocks, left, slots, edge, occ, nb):
    width = slots * edge
    for b in range(nb):
        blocks[b, :, :edge] = coef_ref[:, b * edge : (b + 1) * edge].astype(F32)
    lane = lax.broadcasted_iota(jnp.int32, (1, width), 1) // edge
    direct_parts, mirror_parts = [], []
    direct_target = jnp.full((1, width), -1, jnp.int32)
    mirror_target = jnp.full((1, width), -1, jnp.int32)
    for s in range(slots):
        tile = tile_ref[s]
        first, second = tile // nb, tile % nb
        valid = tile < nb * nb
        keep = jnp.where(valid & (mask_ref[jnp.minimum(tile, nb * nb - 1)] > 0), 1, 0)
        weight = keep.astype(F32)
        mirror = jnp.where(first < second, weight, 0.0)
        direct_parts.append(blocks[jnp.minimum(first, nb - 1)][:, :edge] * weight)
        mirror_parts.append(blocks[second][:, :edge] * mirror)
        direct_target = jnp.where(lane == s, second, direct_target)
        mirror_target = jnp.where(lane == s, first, mirror_target)
    gathered = jnp.concatenate(direct_parts + mirror_parts, axis=1)
    target = jnp.concatenate([direct_target, mirror_target], axis=1)
    row = lax.broadcasted_iota(jnp.int32, (8, 2 * width), 0)
    for half in range(2):
        for core in range(2):
            block = row + core * (8 - half)
            hit = target == block
            rows = []
            for i in range(occ):
                rows.append(jnp.where(hit, gathered[i : i + 1, :], 0.0).astype(BF16))
            left[half, pl.ds(core * 8 * occ, 8 * occ), :] = jnp.concatenate(rows, axis=0)


def second_factor(lam_ref, pairs, occ):
    lams = lam_ref.shape[1]
    rows_l = lax.broadcasted_iota(jnp.int32, (lams, pairs), 0)
    cols_l = lax.broadcasted_iota(jnp.int32, (lams, pairs), 1)
    widen = jnp.where(rows_l == cols_l // SW, 1.0, 0.0).astype(BF16)
    by_pair = jnp.dot(lam_ref[...], widen, preferred_element_type=F32)
    rows_j = lax.broadcasted_iota(jnp.int32, (occ * SW, occ), 0)
    cols_j = lax.broadcasted_iota(jnp.int32, (occ * SW, occ), 1)
    repeat = jnp.where(rows_j // SW == cols_j, 1.0, 0.0).astype(BF16)
    by_row = jnp.dot(repeat, by_pair.astype(BF16), preferred_element_type=F32)
    rows_s = lax.broadcasted_iota(jnp.int32, (occ * SW, pairs), 0)
    cols_s = lax.broadcasted_iota(jnp.int32, (occ * SW, pairs), 1)
    lam_mat = jnp.where(rows_s % SW == cols_s % SW, by_row, 0.0).astype(BF16)
    return jnp.concatenate([lam_mat, lam_mat], axis=1)


def output_order(order, z, edge):
    shape = order.shape
    k = lax.broadcasted_iota(jnp.int32, shape, 0)
    n = lax.broadcasted_iota(jnp.int32, shape, 1)
    tile, lane = k // 128, k % 128
    block = lane % 8
    wide = (lane // 64) * (edge // 2) + (lane // 8) % 8 + 8 * tile
    narrow = (lane // 32) % 2 * (edge // 2) + (lane // 8) % 4 + 16
    narrow = jnp.where(lane // 64 == z // 8, narrow, -1024)
    column = block * edge + jnp.where(tile < 2, wide, narrow)
    order[...] = jnp.where(column == n, 1.0, 0.0).astype(BF16)


def kernel(
    eri_hbm, tile_hbm, mask_hbm, coef_hbm, lam_hbm, out_ref,
    tile_ref, mask_ref, coef_ref, lam_ref, ebuf, eturn, blocks, left, order, acc_a, acc_b, acc_c,
    theirs_p, theirs_q, mine_p, mine_q, core_p, core_q, send_p, send_q, got_p, got_q, send_z, got_z,
    load_sem, small_sem, core_send, core_recv, plane_send, plane_recv, z_send, z_recv, told,
):
    slots, edge, unused, pairs = ebuf.shape
    occ, basis = coef_ref.shape
    nb = basis // edge
    half_edge = edge // 2
    row, col = lax.axis_index("row"), lax.axis_index("col")
    core, orbital = row % 2, row // 2
    jhi, z = col // 16, col % 16
    place = orbital * 2 + jhi
    sibling = (orbital * 2 + 1 - core, col)

    smalls = [
        pltpu.make_async_copy(a, b, small_sem.at[n])
        for n, (a, b) in enumerate(
            [(tile_hbm, tile_ref), (mask_hbm, mask_ref), (coef_hbm, coef_ref), (lam_hbm, lam_ref)]
        )
    ]
    for copy in smalls:
        copy.start()
    loads = [pltpu.make_async_copy(eri_hbm.at[s], ebuf.at[s], load_sem.at[s]) for s in range(slots)]
    for copy in loads:
        copy.start()

    barrier = pltpu.get_barrier_semaphore()

    def greet(d, unused):
        other = place ^ d
        pl.semaphore_signal(
            barrier, inc=1, device_id=((other // 2) * 2, (other % 2) * 16 + z), device_id_type=MESH
        )
        pl.semaphore_signal(
            barrier, inc=1, device_id=(orbital * 2 + 1, jhi * 16 + (z ^ d)), device_id_type=MESH
        )
        return unused

    lax.fori_loop(1, 16, greet, 0)

    @pl.when(core == 1)
    def _():
        pl.semaphore_signal(barrier, inc=1, device_id=sibling, device_id_type=MESH)

    def hear(teller, count):
        @pl.when(core == teller)
        def _():
            pl.semaphore_wait(barrier, count)
            pl.semaphore_signal(told, inc=1, device_id=sibling, device_id_type=MESH)

        @pl.when(core != teller)
        def _():
            pl.semaphore_wait(told, 1)

    output_order(order, z, edge)
    for copy in smalls:
        copy.wait()
    spread_coefficients(tile_ref, mask_ref, coef_ref, blocks, left, slots, edge, occ, nb)
    lam_twice = second_factor(lam_ref, pairs, occ)

    for s in range(slots):
        loads[s].wait()
        eturn[:, s * edge : (s + 1) * edge, :] = jnp.swapaxes(ebuf[s], 0, 1)

    def transform(acc, first, count):
        for half in range(2):
            for step in range(0, count, 2):
                base = half * half_edge + first + step
                right = jnp.concatenate(
                    [
                        jnp.concatenate([eturn[u], ebuf[:, u].reshape(slots * edge, pairs)], axis=0)
                        for u in (base, base + 1)
                    ],
                    axis=1,
                )
                sums = jnp.dot(left[half], right, preferred_element_type=F32)
                for c in range(2):
                    start = ((half ^ c) * count + step) * 8
                    for i in range(occ):
                        g = (c * occ + i) * 8
                        at = i * 2 * count * 8 + start
                        acc[c, at : at + 8, :] = sums[g : g + 8, :pairs]
                        acc[c, at + 8 : at + 16, :] = sums[g : g + 8, pairs:]

    def contract(acc, c, n):
        value = acc[c, n * 256 : n * 256 + 256, :]
        high = value.astype(BF16)
        low = (value - high.astype(F32)).astype(BF16)
        right = jnp.concatenate([high, low], axis=1)
        return lax.dot_general(lam_twice, right, (((1,), (1,)), ((), ())), preferred_element_type=F32)

    def contract_wide(acc, c, dest):
        for n in range(occ // 2):
            got = contract(acc, c, n)
            for k in range(2):
                for h in range(2):
                    dest[4 * n + 2 * k + h, 0:16, :] = got[16 * h : 16 * h + 16, 128 * k : 128 * k + 128]

    def contract_narrow(acc, c, dest):
        low_lanes = lax.broadcasted_iota(jnp.int32, (8, 128), 1) < 64
        for n in range(occ // 4):
            got = contract(acc, c, n)
            for k in range(2):
                for h in range(2):
                    below = got[16 * h : 16 * h + 8, 128 * k : 128 * k + 128]
                    above = got[16 * h + 8 : 16 * h + 16, 128 * k : 128 * k + 128]
                    m = 8 * n + 4 * k + h
                    dest[m, 16:24, :] = jnp.where(low_lanes, below, pltpu.roll(above, 64, 1))
                    dest[m + 2, 16:24, :] = jnp.where(low_lanes, pltpu.roll(below, 64, 1), above)

    def swap_cores(source, dest, n):
        copy = pltpu.make_async_remote_copy(
            src_ref=source, dst_ref=dest, send_sem=core_send.at[n], recv_sem=core_recv.at[n],
            device_id=sibling, device_id_type=MESH,
        )
        copy.start()
        return copy

    def to_plane(send, got, n, slot, other):
        return pltpu.make_async_remote_copy(
            src_ref=send.at[slot],
            dst_ref=got.at[slot],
            send_sem=plane_send.at[n],
            recv_sem=plane_recv.at[n],
            device_id=((other // 2) * 2 + core, (other % 2) * 16 + z),
            device_id_type=MESH,
        )

    def share(mine, theirs, send, got, n):
        for d in PLANE_ORDER:
            other = place ^ d
            send[d] = mine[other] + theirs[other]
            to_plane(send, got, n, d, other).start()
        return to_plane(send, got, n, pl.ds(1, 15), place ^ 1)

    def gather(mine, theirs, got, copies):
        total = mine[place] + theirs[place]
        copies.wait_recv()
        for d in range(1, 16):
            total = total + got[d]
        return total

    transform(acc_a, 0, 8)
    contract_wide(acc_a, 1 - core, theirs_p)
    hear(0, 31)
    first_swap = swap_cores(theirs_p, core_p, 0)
    contract_wide(acc_a, core, mine_p)
    transform(acc_b, 8, 8)
    transform(acc_c, 16, 4)
    contract_wide(acc_b, 1 - core, theirs_q)
    contract_narrow(acc_c, 1 - core, theirs_q)
    second_swap = swap_cores(theirs_q, core_q, 1)
    first_swap.wait_recv()
    p_copies = share(mine_p, core_p, send_p, got_p, 0)
    contract_wide(acc_b, core, mine_q)
    contract_narrow(acc_c, core, mine_q)
    second_swap.wait_recv()
    q_copies = share(mine_q, core_q, send_q, got_q, 1)

    total = gather(mine_p, core_p, got_p, p_copies)
    send_z[:, 0, :] = total
    total = gather(mine_q, core_q, got_q, q_copies)
    send_z[:, 1, :] = total[:16]
    send_z[0:8, 2, :] = total[16:]
    send_z[8:16, 2, :] = total[16:]

    def along_z(source, slot, other):
        return pltpu.make_async_remote_copy(
            src_ref=send_z.at[source],
            dst_ref=got_z.at[slot],
            send_sem=z_send,
            recv_sem=z_recv,
            device_id=(row, jhi * 16 + other),
            device_id_type=MESH,
        )

    hear(1, 30)
    for d in Z_ORDER:
        other = (z + d) % 16
        along_z(other, d, other).start()
    z_copies = along_z(pl.ds(1, 15), pl.ds(1, 15), (z + 1) % 16)
    final = send_z[z]
    z_copies.wait_recv()
    for d in range(1, 16):
        final = final + got_z[d]
    flat = jnp.concatenate([final[k : k + 1, :] for k in range(3)], axis=1)
    high = flat.astype(BF16)
    rest = flat - high.astype(F32)
    middle = rest.astype(BF16)
    low = (rest - middle.astype(F32)).astype(BF16)
    terms = jnp.concatenate([high, middle, low], axis=0)
    picked = jnp.dot(terms, order[...], preferred_element_type=F32)
    out_ref[...] = (picked[0:1] + picked[1:2] + picked[2:3])[:, : out_ref.shape[1]]
    for copy in (first_swap, second_swap, p_copies, q_copies, z_copies):
        copy.wait_send()


def per_device(eri, slot_tile, tile_mask, coef_mu, coef_lam):
    slots, edge, unused, pairs = eri.shape
    basis, occ = coef_mu.shape
    nb = basis // edge
    return pl.pallas_call(
        kernel,
        out_shape=pltpu.VMEM((1, 300), F32),
        in_specs=[pl.BlockSpec(memory_space=pltpu.HBM)] * 5,
        out_specs=pl.BlockSpec(memory_space=pltpu.VMEM),
        scratch_shapes=[
            pltpu.SMEM(slot_tile.shape, jnp.int32),
            pltpu.SMEM(tile_mask.shape, jnp.int32),
            pltpu.VMEM((occ, basis), BF16),
            pltpu.VMEM((occ, coef_lam.shape[0]), BF16),
            pltpu.VMEM((slots, edge, edge, pairs), BF16),
            pltpu.VMEM((edge, slots * edge, pairs), BF16),
            pltpu.VMEM((nb, occ, 128), F32),
            pltpu.VMEM((2, 16 * occ, 2 * slots * edge), BF16),
            pltpu.VMEM((384, 384), BF16),
            pltpu.VMEM((2, occ * 128, pairs), F32),
            pltpu.VMEM((2, occ * 128, pairs), F32),
            pltpu.VMEM((2, occ * 64, pairs), F32),
        ]
        + [pltpu.VMEM((16, height, 128), F32) for unused in range(5) for height in (16, 24)]
        + [
            pltpu.VMEM((16, 3, 128), F32),
            pltpu.VMEM((16, 3, 128), F32),
            pltpu.SemaphoreType.DMA((slots,)),
            pltpu.SemaphoreType.DMA((4,)),
            pltpu.SemaphoreType.DMA((2,)),
            pltpu.SemaphoreType.DMA((2,)),
            pltpu.SemaphoreType.DMA((2,)),
            pltpu.SemaphoreType.DMA((2,)),
            pltpu.SemaphoreType.DMA,
            pltpu.SemaphoreType.DMA,
            pltpu.SemaphoreType.REGULAR,
        ],
        compiler_params=pltpu.CompilerParams(
            collective_id=0, has_side_effects=True, vmem_limit_bytes=56 * 2**20
        ),
    )(eri, slot_tile, tile_mask, coef_mu.T, coef_lam.T)


def solution(mesh):
    in_specs = (P("row", None, None, "col"), P("row"), P(), P(), P("col", None))
    out_specs = P("col", "row")
    return jax.shard_map(
        per_device, mesh=mesh, in_specs=in_specs, out_specs=out_specs, check_vma=False
    )
```

```python
import functools

import jax
import jax.numpy as jnp
from jax import lax
from jax.experimental import pallas as pl
from jax.experimental.pallas import tpu as pltpu
from jax.sharding import PartitionSpec as P

MESH = pl.DeviceIdType.MESH
SW = 4
PLANE_HOPS = (0, 1, 2, 1)
PLANE_ORDER = sorted(
    range(1, 16), key=lambda d: -(PLANE_HOPS[d // 8 * 2 + d % 2] + PLANE_HOPS[d // 2 % 4])
)
Z_ORDER = [8, 7, 9, 6, 10, 5, 11, 4, 12, 3, 13, 2, 14, 1, 15]
F32 = jnp.float32
BF16 = jnp.bfloat16


def spread_coefficients(tile_ref, mask_ref, coef_ref, blocks, left, slots, edge, occ, nb):
    width = slots * edge
    for b in range(nb):
        blocks[b, :, :edge] = coef_ref[:, b * edge : (b + 1) * edge].astype(F32)
    lane = lax.broadcasted_iota(jnp.int32, (1, width), 1) // edge
    direct_parts, mirror_parts = [], []
    direct_target = jnp.full((1, width), -1, jnp.int32)
    mirror_target = jnp.full((1, width), -1, jnp.int32)
    for s in range(slots):
        tile = tile_ref[s]
        first, second = tile // nb, tile % nb
        valid = tile < nb * nb
        keep = jnp.where(valid & (mask_ref[jnp.minimum(tile, nb * nb - 1)] > 0), 1, 0)
        weight = keep.astype(F32)
        mirror = jnp.where(first < second, weight, 0.0)
        direct_parts.append(blocks[jnp.minimum(first, nb - 1)][:, :edge] * weight)
        mirror_parts.append(blocks[second][:, :edge] * mirror)
        direct_target = jnp.where(lane == s, second, direct_target)
        mirror_target = jnp.where(lane == s, first, mirror_target)
    gathered = jnp.concatenate(direct_parts + mirror_parts, axis=1)
    target = jnp.concatenate([direct_target, mirror_target], axis=1)
    row = lax.broadcasted_iota(jnp.int32, (8, 2 * width), 0)
    for half in range(2):
        for core in range(2):
            block = row + core * (8 - half)
            hit = target == block
            rows = []
            for i in range(occ):
                rows.append(jnp.where(hit, gathered[i : i + 1, :], 0.0).astype(BF16))
            left[half, pl.ds(core * 8 * occ, 8 * occ), :] = jnp.concatenate(rows, axis=0)


def second_factor(lam_ref, pairs, occ):
    lams = lam_ref.shape[1]
    rows_l = lax.broadcasted_iota(jnp.int32, (lams, pairs), 0)
    cols_l = lax.broadcasted_iota(jnp.int32, (lams, pairs), 1)
    widen = jnp.where(rows_l == cols_l // SW, 1.0, 0.0).astype(BF16)
    by_pair = jnp.dot(lam_ref[...], widen, preferred_element_type=F32)
    rows_j = lax.broadcasted_iota(jnp.int32, (occ * SW, occ), 0)
    cols_j = lax.broadcasted_iota(jnp.int32, (occ * SW, occ), 1)
    repeat = jnp.where(rows_j // SW == cols_j, 1.0, 0.0).astype(BF16)
    by_row = jnp.dot(repeat, by_pair.astype(BF16), preferred_element_type=F32)
    rows_s = lax.broadcasted_iota(jnp.int32, (occ * SW, pairs), 0)
    cols_s = lax.broadcasted_iota(jnp.int32, (occ * SW, pairs), 1)
    lam_mat = jnp.where(rows_s % SW == cols_s % SW, by_row, 0.0).astype(BF16)
    return jnp.concatenate([lam_mat, lam_mat], axis=1)


def output_order(order, z, edge):
    shape = order.shape
    k = lax.broadcasted_iota(jnp.int32, shape, 0)
    n = lax.broadcasted_iota(jnp.int32, shape, 1)
    tile, lane = k // 128, k % 128
    block = lane % 8
    wide = (lane // 64) * (edge // 2) + (lane // 8) % 8 + 8 * tile
    narrow = (lane // 32) % 2 * (edge // 2) + (lane // 8) % 4 + 16
    narrow = jnp.where(lane // 64 == z // 8, narrow, -1024)
    column = block * edge + jnp.where(tile < 2, wide, narrow)
    order[...] = jnp.where(column == n, 1.0, 0.0).astype(BF16)


def kernel(
    eri_hbm, tile_hbm, mask_hbm, coef_hbm, lam_hbm, out_ref,
    tile_ref, mask_ref, coef_ref, lam_ref, ebuf, eturn, blocks, left, order, acc_a, acc_b, acc_c,
    theirs_p, theirs_q, mine_p, mine_q, core_p, core_q, send_p, send_q, got_p, got_q, send_z, got_z,
    load_sem, small_sem, core_send, core_recv, plane_send, plane_recv, z_send, z_recv, told,
):
    slots, edge, unused, pairs = ebuf.shape
    occ, basis = coef_ref.shape
    nb = basis // edge
    half_edge = edge // 2
    row, col = lax.axis_index("row"), lax.axis_index("col")
    core, orbital = row % 2, row // 2
    jhi, z = col // 16, col % 16
    place = orbital * 2 + jhi
    sibling = (orbital * 2 + 1 - core, col)

    smalls = [
        pltpu.make_async_copy(a, b, small_sem.at[n])
        for n, (a, b) in enumerate(
            [(tile_hbm, tile_ref), (mask_hbm, mask_ref), (coef_hbm, coef_ref), (lam_hbm, lam_ref)]
        )
    ]
    for copy in smalls:
        copy.start()
    loads = [pltpu.make_async_copy(eri_hbm.at[s], ebuf.at[s], load_sem.at[s]) for s in range(slots)]
    for n, copy in enumerate(loads):
        copy.start(priority=int(n >= 4))

    barrier = pltpu.get_barrier_semaphore()

    for d in PLANE_ORDER:
        other = place ^ d
        pl.semaphore_signal(
            barrier, inc=1, device_id=((other // 2) * 2, (other % 2) * 16 + z), device_id_type=MESH
        )

    @pl.when(core == 1)
    def _():
        pl.semaphore_signal(barrier, inc=1, device_id=sibling, device_id_type=MESH)

    def greet(d, unused):
        pl.semaphore_signal(
            barrier, inc=1, device_id=(orbital * 2 + 1, jhi * 16 + (z + d) % 16), device_id_type=MESH
        )
        return unused

    lax.fori_loop(1, 16, greet, 0)

    def hear(teller, count):
        @pl.when(core == teller)
        def _():
            pl.semaphore_wait(barrier, count)
            pl.semaphore_signal(told, inc=1, device_id=sibling, device_id_type=MESH)

        @pl.when(core != teller)
        def _():
            pl.semaphore_wait(told, 1)

    output_order(order, z, edge)
    for copy in smalls:
        copy.wait()
    spread_coefficients(tile_ref, mask_ref, coef_ref, blocks, left, slots, edge, occ, nb)
    lam_twice = second_factor(lam_ref, pairs, occ)

    for s in range(slots):
        loads[s].wait()
        eturn[:, s * edge : (s + 1) * edge, :] = jnp.swapaxes(ebuf[s], 0, 1)

    def transform(acc, first, count):
        for half in range(2):
            for step in range(0, count, 2):
                base = half * half_edge + first + step
                right = jnp.concatenate(
                    [
                        jnp.concatenate([eturn[u], ebuf[:, u].reshape(slots * edge, pairs)], axis=0)
                        for u in (base, base + 1)
                    ],
                    axis=1,
                )
                sums = jnp.dot(left[half], right, preferred_element_type=F32)
                for c in range(2):
                    start = ((half ^ c) * count + step) * 8
                    for i in range(occ):
                        g = (c * occ + i) * 8
                        at = i * 2 * count * 8 + start
                        acc[c, at : at + 8, :] = sums[g : g + 8, :pairs]
                        acc[c, at + 8 : at + 16, :] = sums[g : g + 8, pairs:]

    def contract(acc, c, n):
        value = acc[c, n * 256 : n * 256 + 256, :]
        high = value.astype(BF16)
        low = (value - high.astype(F32)).astype(BF16)
        right = jnp.concatenate([high, low], axis=1)
        return lax.dot_general(lam_twice, right, (((1,), (1,)), ((), ())), preferred_element_type=F32)

    def contract_wide(acc, c, dest):
        for n in range(occ // 2):
            got = contract(acc, c, n)
            for k in range(2):
                for h in range(2):
                    dest[4 * n + 2 * k + h, 0:16, :] = got[16 * h : 16 * h + 16, 128 * k : 128 * k + 128]

    def contract_narrow(acc, c, dest):
        low_lanes = lax.broadcasted_iota(jnp.int32, (8, 128), 1) < 64
        for n in range(occ // 4):
            got = contract(acc, c, n)
            for k in range(2):
                for h in range(2):
                    below = got[16 * h : 16 * h + 8, 128 * k : 128 * k + 128]
                    above = got[16 * h + 8 : 16 * h + 16, 128 * k : 128 * k + 128]
                    m = 8 * n + 4 * k + h
                    dest[m, 16:24, :] = jnp.where(low_lanes, below, pltpu.roll(above, 64, 1))
                    dest[m + 2, 16:24, :] = jnp.where(low_lanes, pltpu.roll(below, 64, 1), above)

    def swap_cores(source, dest, n):
        copy = pltpu.make_async_remote_copy(
            src_ref=source, dst_ref=dest, send_sem=core_send.at[n], recv_sem=core_recv.at[n],
            device_id=sibling, device_id_type=MESH,
        )
        copy.start()
        return copy

    def to_plane(send, got, n, slot, other):
        return pltpu.make_async_remote_copy(
            src_ref=send.at[slot],
            dst_ref=got.at[slot],
            send_sem=plane_send.at[n],
            recv_sem=plane_recv.at[n],
            device_id=((other // 2) * 2 + core, (other % 2) * 16 + z),
            device_id_type=MESH,
        )

    def share(mine, theirs, send, got, n):
        def give(slot, other):
            send[slot] = mine[other] + theirs[other]
            to_plane(send, got, n, slot, other).start()

        @pl.when(place != 0)
        def _():
            give(place, 0)

        for d in PLANE_ORDER:

            @pl.when(place != d)
            def _():
                give(d, place ^ d)

        return to_plane(send, got, n, pl.ds(1, 15), place ^ 1)

    def gather(mine, theirs, got, copies):
        total = mine[place] + theirs[place]
        copies.wait_recv()
        for d in range(1, 16):
            total = total + got[d]
        return total

    transform(acc_a, 0, 8)
    contract_wide(acc_a, 1 - core, theirs_p)
    hear(0, 31)
    first_swap = swap_cores(theirs_p, core_p, 0)
    contract_wide(acc_a, core, mine_p)
    transform(acc_b, 8, 8)
    transform(acc_c, 16, 4)
    contract_wide(acc_b, 1 - core, theirs_q)
    contract_narrow(acc_c, 1 - core, theirs_q)
    second_swap = swap_cores(theirs_q, core_q, 1)
    first_swap.wait_recv()
    p_copies = share(mine_p, core_p, send_p, got_p, 0)
    contract_wide(acc_b, core, mine_q)
    contract_narrow(acc_c, core, mine_q)
    second_swap.wait_recv()
    q_copies = share(mine_q, core_q, send_q, got_q, 1)

    hear(1, 30)
    total = gather(mine_p, core_p, got_p, p_copies)
    send_z[:, 0, :] = total
    total = gather(mine_q, core_q, got_q, q_copies)
    send_z[:, 1, :] = total[:16]
    send_z[0:8, 2, :] = total[16:]
    send_z[8:16, 2, :] = total[16:]

    def along_z(source, slot, other):
        return pltpu.make_async_remote_copy(
            src_ref=send_z.at[source],
            dst_ref=got_z.at[slot],
            send_sem=z_send,
            recv_sem=z_recv,
            device_id=(row, jhi * 16 + other),
            device_id_type=MESH,
        )

    for d in Z_ORDER:
        other = (z + d) % 16
        along_z(other, d, other).start()
    z_copies = along_z(pl.ds(1, 15), pl.ds(1, 15), (z + 1) % 16)
    final = send_z[z]
    z_copies.wait_recv()
    for d in range(1, 16):
        final = final + got_z[d]
    flat = jnp.concatenate([final[k : k + 1, :] for k in range(3)], axis=1)
    high = flat.astype(BF16)
    rest = flat - high.astype(F32)
    middle = rest.astype(BF16)
    low = (rest - middle.astype(F32)).astype(BF16)
    terms = jnp.concatenate([high, middle, low], axis=0)
    picked = jnp.dot(terms, order[...], preferred_element_type=F32)
    out_ref[...] = (picked[0:1] + picked[1:2] + picked[2:3])[:, : out_ref.shape[1]]
    for copy in (first_swap, second_swap, p_copies, q_copies, z_copies):
        copy.wait_send()


def per_device(eri, slot_tile, tile_mask, coef_mu, coef_lam):
    slots, edge, unused, pairs = eri.shape
    basis, occ = coef_mu.shape
    nb = basis // edge
    return pl.pallas_call(
        kernel,
        out_shape=pltpu.VMEM((1, 300), F32),
        in_specs=[pl.BlockSpec(memory_space=pltpu.HBM)] * 5,
        out_specs=pl.BlockSpec(memory_space=pltpu.VMEM),
        scratch_shapes=[
            pltpu.SMEM(slot_tile.shape, jnp.int32),
            pltpu.SMEM(tile_mask.shape, jnp.int32),
            pltpu.VMEM((occ, basis), BF16),
            pltpu.VMEM((occ, coef_lam.shape[0]), BF16),
            pltpu.VMEM((slots, edge, edge, pairs), BF16),
            pltpu.VMEM((edge, slots * edge, pairs), BF16),
            pltpu.VMEM((nb, occ, 128), F32),
            pltpu.VMEM((2, 16 * occ, 2 * slots * edge), BF16),
            pltpu.VMEM((384, 384), BF16),
            pltpu.VMEM((2, occ * 128, pairs), F32),
            pltpu.VMEM((2, occ * 128, pairs), F32),
            pltpu.VMEM((2, occ * 64, pairs), F32),
        ]
        + [pltpu.VMEM((16, height, 128), F32) for unused in range(5) for height in (16, 24)]
        + [
            pltpu.VMEM((16, 3, 128), F32),
            pltpu.VMEM((16, 3, 128), F32),
            pltpu.SemaphoreType.DMA((slots,)),
            pltpu.SemaphoreType.DMA((4,)),
            pltpu.SemaphoreType.DMA((2,)),
            pltpu.SemaphoreType.DMA((2,)),
            pltpu.SemaphoreType.DMA((2,)),
            pltpu.SemaphoreType.DMA((2,)),
            pltpu.SemaphoreType.DMA,
            pltpu.SemaphoreType.DMA,
            pltpu.SemaphoreType.REGULAR,
        ],
        compiler_params=pltpu.CompilerParams(
            collective_id=0, has_side_effects=True, vmem_limit_bytes=56 * 2**20
        ),
    )(eri, slot_tile, tile_mask, coef_mu.T, coef_lam.T)


def solution(mesh):
    in_specs = (P("row", None, None, "col"), P("row"), P(), P(), P("col", None))
    out_specs = P("col", "row")
    return jax.shard_map(
        per_device, mesh=mesh, in_specs=in_specs, out_specs=out_specs, check_vma=False
    )
```

```python
import functools

import jax
import jax.numpy as jnp
from jax import lax
from jax.experimental import pallas as pl
from jax.experimental.pallas import tpu as pltpu
from jax.sharding import PartitionSpec as P

MESH = pl.DeviceIdType.MESH
SW = 4
PLANE_HOPS = (0, 1, 2, 1)
PLANE_ORDER = sorted(
    range(1, 16), key=lambda d: -(PLANE_HOPS[d // 8 * 2 + d % 2] + PLANE_HOPS[d // 2 % 4])
)
Z_ORDER = [8, 7, 9, 6, 10, 5, 11, 4, 12, 3, 13, 2, 14, 1, 15]
F32 = jnp.float32
BF16 = jnp.bfloat16


def spread_coefficients(tile_ref, mask_ref, coef_ref, blocks, left, slots, edge, occ, nb):
    width = slots * edge
    for b in range(nb):
        blocks[b, :, :edge] = coef_ref[:, b * edge : (b + 1) * edge].astype(F32)
    lane = lax.broadcasted_iota(jnp.int32, (1, width), 1) // edge
    direct_parts, mirror_parts = [], []
    direct_target = jnp.full((1, width), -1, jnp.int32)
    mirror_target = jnp.full((1, width), -1, jnp.int32)
    for s in range(slots):
        tile = tile_ref[s]
        first, second = tile // nb, tile % nb
        valid = tile < nb * nb
        keep = jnp.where(valid & (mask_ref[jnp.minimum(tile, nb * nb - 1)] > 0), 1, 0)
        weight = keep.astype(F32)
        mirror = jnp.where(first < second, weight, 0.0)
        direct_parts.append(blocks[jnp.minimum(first, nb - 1)][:, :edge] * weight)
        mirror_parts.append(blocks[second][:, :edge] * mirror)
        direct_target = jnp.where(lane == s, second, direct_target)
        mirror_target = jnp.where(lane == s, first, mirror_target)
    gathered = jnp.concatenate(direct_parts + mirror_parts, axis=1)
    target = jnp.concatenate([direct_target, mirror_target], axis=1)
    row = lax.broadcasted_iota(jnp.int32, (8, 2 * width), 0)
    for half in range(2):
        for core in range(2):
            block = row + core * (8 - half)
            hit = target == block
            rows = []
            for i in range(occ):
                rows.append(jnp.where(hit, gathered[i : i + 1, :], 0.0).astype(BF16))
            left[half, pl.ds(core * 8 * occ, 8 * occ), :] = jnp.concatenate(rows, axis=0)


def second_factor(lam_ref, pairs, occ):
    lams = lam_ref.shape[1]
    rows_l = lax.broadcasted_iota(jnp.int32, (lams, pairs), 0)
    cols_l = lax.broadcasted_iota(jnp.int32, (lams, pairs), 1)
    widen = jnp.where(rows_l == cols_l // SW, 1.0, 0.0).astype(BF16)
    by_pair = jnp.dot(lam_ref[...], widen, preferred_element_type=F32)
    rows_j = lax.broadcasted_iota(jnp.int32, (occ * SW, occ), 0)
    cols_j = lax.broadcasted_iota(jnp.int32, (occ * SW, occ), 1)
    repeat = jnp.where(rows_j // SW == cols_j, 1.0, 0.0).astype(BF16)
    by_row = jnp.dot(repeat, by_pair.astype(BF16), preferred_element_type=F32)
    rows_s = lax.broadcasted_iota(jnp.int32, (occ * SW, pairs), 0)
    cols_s = lax.broadcasted_iota(jnp.int32, (occ * SW, pairs), 1)
    lam_mat = jnp.where(rows_s % SW == cols_s % SW, by_row, 0.0).astype(BF16)
    return jnp.concatenate([lam_mat, lam_mat], axis=1)


def output_order(order, z, edge):
    shape = order.shape
    k = lax.broadcasted_iota(jnp.int32, shape, 0)
    n = lax.broadcasted_iota(jnp.int32, shape, 1)
    tile, lane = k // 128, k % 128
    block = lane % 8
    wide = (lane // 64) * (edge // 2) + (lane // 8) % 8 + 8 * tile
    narrow = (lane // 32) % 2 * (edge // 2) + (lane // 8) % 4 + 16
    narrow = jnp.where(lane // 64 == z // 8, narrow, -1024)
    column = block * edge + jnp.where(tile < 2, wide, narrow)
    order[...] = jnp.where(column == n, 1.0, 0.0).astype(BF16)


def kernel(
    eri_hbm, tile_hbm, mask_hbm, coef_hbm, lam_hbm, out_ref,
    tile_ref, mask_ref, coef_ref, lam_ref, ebuf, eturn, blocks, left, order, acc_a, acc_b, acc_c,
    theirs_p, theirs_q, mine_p, mine_q, core_p, core_q, send_p, send_q, got_p, got_q, send_z, got_z,
    load_sem, small_sem, core_send, core_recv, plane_send, plane_recv, z_send, z_recv, told,
):
    slots, edge, unused, pairs = ebuf.shape
    occ, basis = coef_ref.shape
    nb = basis // edge
    half_edge = edge // 2
    row, col = lax.axis_index("row"), lax.axis_index("col")
    core, orbital = row % 2, row // 2
    jhi, z = col // 16, col % 16
    place = orbital * 2 + jhi
    sibling = (orbital * 2 + 1 - core, col)

    smalls = [
        pltpu.make_async_copy(a, b, small_sem.at[n])
        for n, (a, b) in enumerate(
            [(tile_hbm, tile_ref), (mask_hbm, mask_ref), (coef_hbm, coef_ref), (lam_hbm, lam_ref)]
        )
    ]
    for copy in smalls:
        copy.start()
    group = slots // 2

    def load(n, first, count):
        return pltpu.make_async_copy(
            eri_hbm.at[pl.ds(first, count)], ebuf.at[pl.ds(first, count)], load_sem.at[n]
        )

    for n in range(2):
        for s in range(group):
            load(n, n * group + s, 1).start(priority=n)

    barrier = pltpu.get_barrier_semaphore()

    for d in PLANE_ORDER:
        other = place ^ d
        pl.semaphore_signal(
            barrier, inc=1, device_id=((other // 2) * 2, (other % 2) * 16 + z), device_id_type=MESH
        )

    @pl.when(core == 1)
    def _():
        pl.semaphore_signal(barrier, inc=1, device_id=sibling, device_id_type=MESH)

    def greet(d, unused):
        pl.semaphore_signal(
            barrier, inc=1, device_id=(orbital * 2 + 1, jhi * 16 + (z + d) % 16), device_id_type=MESH
        )
        return unused

    lax.fori_loop(1, 16, greet, 0)

    def hear(teller, count):
        @pl.when(core == teller)
        def _():
            pl.semaphore_wait(barrier, count)
            pl.semaphore_signal(told, inc=1, device_id=sibling, device_id_type=MESH)

        @pl.when(core != teller)
        def _():
            pl.semaphore_wait(told, 1)

    output_order(order, z, edge)
    for copy in smalls:
        copy.wait()
    spread_coefficients(tile_ref, mask_ref, coef_ref, blocks, left, slots, edge, occ, nb)
    lam_twice = second_factor(lam_ref, pairs, occ)

    for s in range(slots):
        if s % group == 0:
            load(s // group, s, group).wait()
        eturn[:, s * edge : (s + 1) * edge, :] = jnp.swapaxes(ebuf[s], 0, 1)

    def transform(acc, first, count):
        for half in range(2):
            for step in range(0, count, 2):
                base = half * half_edge + first + step
                right = jnp.concatenate(
                    [
                        jnp.concatenate([eturn[u], ebuf[:, u].reshape(slots * edge, pairs)], axis=0)
                        for u in (base, base + 1)
                    ],
                    axis=1,
                )
                sums = jnp.dot(left[half], right, preferred_element_type=F32)
                for c in range(2):
                    start = ((half ^ c) * count + step) * 8
                    for i in range(occ):
                        g = (c * occ + i) * 8
                        at = i * 2 * count * 8 + start
                        acc[c, at : at + 8, :] = sums[g : g + 8, :pairs]
                        acc[c, at + 8 : at + 16, :] = sums[g : g + 8, pairs:]

    def contract(acc, c, n):
        value = acc[c, n * 256 : n * 256 + 256, :]
        high = value.astype(BF16)
        low = (value - high.astype(F32)).astype(BF16)
        right = jnp.concatenate([high, low], axis=1)
        return lax.dot_general(lam_twice, right, (((1,), (1,)), ((), ())), preferred_element_type=F32)

    def contract_wide(acc, c, dest):
        for n in range(occ // 2):
            got = contract(acc, c, n)
            for k in range(2):
                for h in range(2):
                    dest[4 * n + 2 * k + h, 0:16, :] = got[16 * h : 16 * h + 16, 128 * k : 128 * k + 128]

    def contract_narrow(acc, c, dest):
        low_lanes = lax.broadcasted_iota(jnp.int32, (8, 128), 1) < 64
        for n in range(occ // 4):
            got = contract(acc, c, n)
            for k in range(2):
                for h in range(2):
                    below = got[16 * h : 16 * h + 8, 128 * k : 128 * k + 128]
                    above = got[16 * h + 8 : 16 * h + 16, 128 * k : 128 * k + 128]
                    m = 8 * n + 4 * k + h
                    dest[m, 16:24, :] = jnp.where(low_lanes, below, pltpu.roll(above, 64, 1))
                    dest[m + 2, 16:24, :] = jnp.where(low_lanes, pltpu.roll(below, 64, 1), above)

    def swap_cores(source, dest, n):
        copy = pltpu.make_async_remote_copy(
            src_ref=source, dst_ref=dest, send_sem=core_send.at[n], recv_sem=core_recv.at[n],
            device_id=sibling, device_id_type=MESH,
        )
        copy.start()
        return copy

    def to_plane(send, got, n, slot, other):
        return pltpu.make_async_remote_copy(
            src_ref=send.at[slot],
            dst_ref=got.at[slot],
            send_sem=plane_send.at[n],
            recv_sem=plane_recv.at[n],
            device_id=((other // 2) * 2 + core, (other % 2) * 16 + z),
            device_id_type=MESH,
        )

    def share(mine, theirs, send, got, n):
        def give(slot, other):
            send[slot] = mine[other] + theirs[other]
            to_plane(send, got, n, slot, other).start()

        @pl.when(place != 0)
        def _():
            give(place, 0)

        for d in PLANE_ORDER:

            @pl.when(place != d)
            def _():
                give(d, place ^ d)

        return to_plane(send, got, n, pl.ds(1, 15), place ^ 1)

    def gather(mine, theirs, got, copies):
        total = mine[place] + theirs[place]
        copies.wait_recv()
        for d in range(1, 16):
            total = total + got[d]
        return total

    transform(acc_a, 0, 8)
    contract_wide(acc_a, 1 - core, theirs_p)
    contract_wide(acc_a, core, mine_p)
    hear(0, 31)
    first_swap = swap_cores(theirs_p, core_p, 0)
    transform(acc_b, 8, 8)
    transform(acc_c, 16, 4)
    contract_wide(acc_b, 1 - core, theirs_q)
    contract_narrow(acc_c, 1 - core, theirs_q)
    second_swap = swap_cores(theirs_q, core_q, 1)
    first_swap.wait_recv()
    p_copies = share(mine_p, core_p, send_p, got_p, 0)
    contract_wide(acc_b, core, mine_q)
    contract_narrow(acc_c, core, mine_q)
    second_swap.wait_recv()
    q_copies = share(mine_q, core_q, send_q, got_q, 1)

    hear(1, 30)
    total = gather(mine_p, core_p, got_p, p_copies)
    send_z[:, 0, :] = total
    total = gather(mine_q, core_q, got_q, q_copies)
    send_z[:, 1, :] = total[:16]
    send_z[0:8, 2, :] = total[16:]
    send_z[8:16, 2, :] = total[16:]

    def along_z(source, slot, other):
        return pltpu.make_async_remote_copy(
            src_ref=send_z.at[source],
            dst_ref=got_z.at[slot],
            send_sem=z_send,
            recv_sem=z_recv,
            device_id=(row, jhi * 16 + other),
            device_id_type=MESH,
        )

    for d in Z_ORDER:
        other = (z + d) % 16
        along_z(other, d, other).start()
    z_copies = along_z(pl.ds(1, 15), pl.ds(1, 15), (z + 1) % 16)
    final = send_z[z]
    z_copies.wait_recv()
    for d in range(1, 16):
        final = final + got_z[d]
    flat = jnp.concatenate([final[k : k + 1, :] for k in range(3)], axis=1)
    high = flat.astype(BF16)
    rest = flat - high.astype(F32)
    middle = rest.astype(BF16)
    low = (rest - middle.astype(F32)).astype(BF16)
    terms = jnp.concatenate([high, middle, low], axis=0)
    picked = jnp.dot(terms, order[...], preferred_element_type=F32)
    out_ref[...] = (picked[0:1] + picked[1:2] + picked[2:3])[:, : out_ref.shape[1]]
    for copy in (first_swap, second_swap, p_copies, q_copies, z_copies):
        copy.wait_send()


def per_device(eri, slot_tile, tile_mask, coef_mu, coef_lam):
    slots, edge, unused, pairs = eri.shape
    basis, occ = coef_mu.shape
    nb = basis // edge
    return pl.pallas_call(
        kernel,
        out_shape=pltpu.VMEM((1, 300), F32),
        in_specs=[pl.BlockSpec(memory_space=pltpu.HBM)] * 5,
        out_specs=pl.BlockSpec(memory_space=pltpu.VMEM),
        scratch_shapes=[
            pltpu.SMEM(slot_tile.shape, jnp.int32),
            pltpu.SMEM(tile_mask.shape, jnp.int32),
            pltpu.VMEM((occ, basis), BF16),
            pltpu.VMEM((occ, coef_lam.shape[0]), BF16),
            pltpu.VMEM((slots, edge, edge, pairs), BF16),
            pltpu.VMEM((edge, slots * edge, pairs), BF16),
            pltpu.VMEM((nb, occ, 128), F32),
            pltpu.VMEM((2, 16 * occ, 2 * slots * edge), BF16),
            pltpu.VMEM((384, 384), BF16),
            pltpu.VMEM((2, occ * 128, pairs), F32),
            pltpu.VMEM((2, occ * 128, pairs), F32),
            pltpu.VMEM((2, occ * 64, pairs), F32),
        ]
        + [pltpu.VMEM((16, height, 128), F32) for unused in range(5) for height in (16, 24)]
        + [
            pltpu.VMEM((16, 3, 128), F32),
            pltpu.VMEM((16, 3, 128), F32),
            pltpu.SemaphoreType.DMA((2,)),
            pltpu.SemaphoreType.DMA((4,)),
            pltpu.SemaphoreType.DMA((2,)),
            pltpu.SemaphoreType.DMA((2,)),
            pltpu.SemaphoreType.DMA((2,)),
            pltpu.SemaphoreType.DMA((2,)),
            pltpu.SemaphoreType.DMA,
            pltpu.SemaphoreType.DMA,
            pltpu.SemaphoreType.REGULAR,
        ],
        compiler_params=pltpu.CompilerParams(
            collective_id=0, has_side_effects=True, vmem_limit_bytes=56 * 2**20
        ),
    )(eri, slot_tile, tile_mask, coef_mu.T, coef_lam.T)


def solution(mesh):
    in_specs = (P("row", None, None, "col"), P("row"), P(), P(), P("col", None))
    out_specs = P("col", "row")
    return jax.shard_map(
        per_device, mesh=mesh, in_specs=in_specs, out_specs=out_specs, check_vma=False
    )
```
